32 devices in a mesh: groups: 1, ep: 32 (over z, y, x, core).
Axes of the slice: x: 2, y: 2, z: 4, core: 2. Of those that a mesh axis runs over, the one named last changes fastest.
Arguments:
- queries: bfloat16 [128, 8, 16, 576], P(('groups', 'ep')), may hold values from -48 to 48
- cache: bfloat16 [128, 384, 576], P(('groups', 'ep')), may hold values from -4 to 4
- drafts: bfloat16 [128, 8, 576], P(('groups', 'ep')), may hold values from -8 to 8
- lengths: int32 [128], P(('groups', 'ep')), may hold values from 96 to 384
- value_up: bfloat16 [16, 512, 128], replicated, may hold values from -0.25 to 0.25
- residual: bfloat16 [1024, 2048], P(('groups', 'ep')), may hold values from -20 to 20
- norm_gain: float32 [2048], replicated, may hold values from 0.5 to 1.5
- w_gate: bfloat16 [32, 2048, 704], P('ep'), may hold values from -0.125 to 0.125
- w_up: bfloat16 [32, 2048, 704], P('ep'), may hold values from -0.125 to 0.125
- w_down: bfloat16 [32, 704, 2048], P('ep'), may hold values from -0.15625 to 0.15625
- routes: int32 [1024, 6], P(('groups', 'ep')), may hold values from 0 to 15, all different within a row; in each aligned block of 32 rows (0 to 31, 32 to 63, ...) at most 14 rows name the same one
- combine_weights: float32 [1024, 6], P(('groups', 'ep')), may hold values from 0.05 to 0.4
Outputs:
- layer_out: bfloat16 [1024, 2048], P(('groups', 'ep'))
The draws below stay inside these ranges and needn't reach their ends.
Inputs may be any that keep to these rules, and one draw needn't show every extreme that they name: `routes`: among the rows of one device, no expert is named more than 14 times over all slots.
All inputs are finite; a program needn't handle non-finite values.
Results may differ from the reference program's by a relative error of at most 0.0043.
Values may be sent and summed in bfloat16 or wider, within the bound.
No kernel may reach another device: no remote copies, remote signals or barrier semaphores. Data moves between devices by JAX's collectives and lax.ppermute only.
A program may use at most 64 MiB of HBM per device.

```python
import math
import jax
import jax.numpy as jnp
import numpy as np
from jax import lax

D = 2048
H = 16
LAT = 512
ROPE = 64
VDIM = 128
FF = 1408
TOP = 6
DRAFT = 8
CACHE = 384
EXPERTS = 16
FF_HALF = 704
TOK_DEV = 32
REQS = 128
TOKENS = 1024
CAP = 14
N_EP = 32


def base_cache(key):
    first = jax.random.fold_in(key, 11)
    shape = (REQS, CACHE, LAT + ROPE)
    values = jnp.clip(jax.random.normal(first, shape, jnp.float32), -4.0, 4.0)
    return values


def draw_cache(key, part):
    values = base_cache(key)
    return jnp.clip(values, -4.0, 4.0).astype(jnp.bfloat16)


def draw_queries(key, part):
    shape = (REQS, DRAFT, H, LAT + ROPE)
    values = jnp.clip(jax.random.normal(jax.random.fold_in(key, 14), shape, jnp.float32), -4.0, 4.0)
    return values.astype(jnp.bfloat16)


def draw_residual(key, part):
    shape = (TOKENS, D)
    rows = jnp.exp(jax.random.uniform(jax.random.fold_in(key, 21), (TOKENS, 1), jnp.float32, -1.386, 0.916))
    columns = jnp.exp(jax.random.uniform(jax.random.fold_in(key, 22), (1, D), jnp.float32, -0.693, 0.693))
    base = jnp.clip(jax.random.normal(jax.random.fold_in(key, 24), shape, jnp.float32), -4.0, 4.0)
    return jnp.clip(base * rows * columns, -20.0, 20.0).astype(jnp.bfloat16)


def with_ends(drawn, own_key, low, largest):
    dims = drawn.shape
    spot = [jax.random.randint(jax.random.fold_in(own_key, axis), (), 0, dims[axis]) for axis in range(len(dims))]
    drawn = drawn.at[tuple(spot)].set(low)
    longest = dims.index(max(dims))
    spot[longest] = (spot[longest] + 1) % dims[longest]
    return drawn.at[tuple(spot)].set(largest)


def block_levels(stream_key, shape, split, least, top_value):
    loudness, own = 1.0, jax.random.fold_in(stream_key, 6)
    for position, parts in split:
        draws = jnp.exp(jax.random.uniform(jax.random.fold_in(own, position), (parts,), jnp.float32, least / len(split), top_value / len(split)))
        loudness = loudness * jnp.repeat(draws, shape[position] // parts).reshape([-1 if axis == position else 1 for axis in range(len(shape))])
    return loudness


def routed_block(stream_key, own, number, rows, count, top, bound, slope):
    ranking = jax.random.permutation(stream_key, count)
    heavy_load, usual = portions_of(count, rows * top, bound, slope, True), portions_of(count, rows * top, bound, slope, False)
    places = jnp.arange(count)

    def named(tallies, turn):
        used = int((tallies > 0).sum())
        fixed = max(1, used // 4)
        shifted = fixed + (places - fixed + turn * (used - fixed)) % max(1, count - fixed)
        return jnp.zeros((count,), jnp.int32).at[ranking[jnp.where(places < fixed, places, shifted)]].set(jnp.asarray(tallies, jnp.int32))

    tallies = jnp.where(number % 4 == 0, named(heavy_load, number // 4), named(usual, number - number // 4 - 1))
    mixed = jax.random.permutation(jax.random.fold_in(own, 3), count)
    donor, taker = mixed[0:count // 2 * 2:2], mixed[1:count // 2 * 2:2]
    slack = jnp.minimum(tallies[donor] - 1, bound - tallies[taker]) // 2
    slack = jnp.where((donor == ranking[0]) | (taker == ranking[0]) | (tallies[taker] == 0), 0, jnp.maximum(slack, 0))
    shifted = jax.random.randint(jax.random.fold_in(own, 4), (count // 2,), 0, 1 << 20) % (slack + 1)
    tallies = tallies.at[donor].add(-shifted).at[taker].add(shifted)
    labels = jnp.searchsorted(jnp.cumsum(tallies), jnp.arange(rows * top), side="right").astype(jnp.int32)
    table = labels.reshape(top, rows).T
    table = table[jax.random.permutation(jax.random.fold_in(own, 1), rows)]
    turn = jax.random.randint(jax.random.fold_in(own, 2), (rows, 1), 0, top)
    return jnp.take_along_axis(table, (jnp.arange(top)[None, :] + turn) % top, axis=1)


def portions_of(number_of, total, most, lean, full):
    loads = [(1 << 20) // math.isqrt(grade ** lean) + 1 for grade in range(1, number_of + 1)]
    largest = most if full else min(most, max(-(-total // number_of), total * loads[0] // sum(loads)))
    least = 1 if total - largest >= number_of - 1 else 0
    holding, rest = [largest] + [least] * (number_of - 1), total - largest - least * (number_of - 1)
    while rest > 0:
        movable = [i for i in range(1, number_of) if holding[i] < largest] or [i for i in range(1, number_of) if holding[i] < most]
        mass, budget = sum([loads[i] for i in movable]), rest
        for i in movable:
            more = min(most - holding[i], max(1, budget * loads[i] // mass), rest)
            holding[i] = holding[i] + more
            rest = rest - more
    return np.array(holding)


def bell_draw(own_key, extent, scale, reach, cuts=(), kind=jnp.bfloat16):
    drawn = scale * jax.random.normal(own_key, extent, jnp.float32)
    if cuts:
        drawn = drawn * block_levels(own_key, extent, cuts, -0.22, 0.18)
    return jnp.clip(drawn, -reach, reach).astype(kind)


def setup_inputs(seed: int = 0, part: int = 0) -> dict:
    streams_of = jax.random.split(jax.random.key(seed), 13)
    part_splits = jax.random.split(jax.random.fold_in(streams_of[12], part), 13)
    queries = draw_queries(jax.random.fold_in(jax.random.fold_in(streams_of[12], part), 71), part)
    cache = draw_cache(jax.random.fold_in(jax.random.fold_in(streams_of[12], part), 71), part)
    drafts = bell_draw(part_splits[2], (REQS, DRAFT, LAT + ROPE), 2.0, 8.0, ((0, 32),))
    lengths = with_ends(jax.random.randint(part_splits[3], (REQS,), CACHE // 4, CACHE + 1), jax.random.fold_in(part_splits[3], 1), CACHE // 4, CACHE).astype(jnp.int32)
    value_up = bell_draw(streams_of[4], (H, LAT, VDIM), LAT ** -0.5, 0.25)
    residual = draw_residual(jax.random.fold_in(jax.random.fold_in(streams_of[12], part), 71), part)
    norm_gain = jnp.clip(1.0 + 0.1 * jax.random.normal(streams_of[6], (D,), jnp.float32), 0.5, 1.5)
    w_gate = bell_draw(streams_of[7], (2 * EXPERTS, D, FF_HALF), D ** -0.5, 0.125, ((0, 32),))
    w_up = bell_draw(streams_of[8], (2 * EXPERTS, D, FF_HALF), D ** -0.5, 0.125, ((0, 32),))
    w_down = bell_draw(streams_of[9], (2 * EXPERTS, FF_HALF, D), FF ** -0.5, 0.15625, ((0, 32),))
    routes_keys = jax.random.split(jax.random.fold_in(part_splits[10], 1), TOKENS // TOK_DEV)
    routes_turns = jax.random.permutation(jax.random.fold_in(part_splits[10], 3), TOKENS // TOK_DEV)
    routes = jax.vmap(lambda own, number: routed_block(jax.random.fold_in(part_splits[10], 2), own, number, TOK_DEV, EXPERTS, TOP, CAP, 2))(routes_keys, routes_turns).reshape((TOKENS, TOP))
    combine_weights = jnp.clip(0.05 + 0.35 * jax.random.uniform(part_splits[11], (TOKENS, TOP), jnp.float32) ** block_levels(part_splits[11], (TOKENS, TOP), ((0, 32),), -0.2, 0.2), 0.05, 0.4)
    return {"queries": queries, "cache": cache, "drafts": drafts, "lengths": lengths, "value_up": value_up, "residual": residual, "norm_gain": norm_gain, "w_gate": w_gate, "w_up": w_up, "w_down": w_down, "routes": routes, "combine_weights": combine_weights}


def attend(queries, cache, drafts, lengths, value_up):
    reqs, draft, heads, width = queries.shape
    latent = value_up.shape[1]
    scale = (VDIM + ROPE) ** (-0.5)
    q_full = queries.astype(jnp.float32)
    c_full = cache.astype(jnp.float32)
    d_full = drafts.astype(jnp.float32)
    cached = jnp.einsum('rjhk,rck->rjhc', q_full, c_full) * scale
    own = jnp.einsum('rjhk,rik->rjhi', q_full, d_full) * scale
    visible = (jnp.arange(cache.shape[1], dtype=jnp.int32)[None, :] < lengths[:, None])[:, None, None, :]
    causal = (jnp.arange(draft, dtype=jnp.int32)[None, :] <= jnp.arange(draft, dtype=jnp.int32)[:, None])[None, :, None, :]
    cached = jnp.where(visible, cached, -1e+30)
    own = jnp.where(causal, own, -1e+30)
    highest = jnp.maximum(lax.optimization_barrier(jnp.max(cached, axis=-1, keepdims=True)), lax.optimization_barrier(jnp.max(own, axis=-1, keepdims=True)))
    e_cached = jnp.where(visible, jnp.exp(cached - highest), 0.0)
    e_own = jnp.where(causal, jnp.exp(own - highest), 0.0)
    total = lax.optimization_barrier(jnp.sum(e_cached, axis=-1, keepdims=True)) + lax.optimization_barrier(jnp.sum(e_own, axis=-1, keepdims=True))
    p_cached = (e_cached / total).astype(jnp.bfloat16).astype(jnp.float32)
    p_own = (e_own / total).astype(jnp.bfloat16).astype(jnp.float32)
    mixed = jnp.einsum('rjhc,rcl->rjhl', p_cached, c_full[..., :latent]) + jnp.einsum('rjhi,ril->rjhl', p_own, d_full[..., :latent])
    mixed = mixed.astype(jnp.bfloat16).astype(jnp.float32)
    heads_out = jnp.einsum('rjhl,hlv->rjhv', mixed, value_up.astype(jnp.float32))
    return heads_out.reshape(reqs * draft, heads * value_up.shape[2])

def run_expert(items):
    rows, gate_w, up_w, down_w = items
    total = jnp.zeros((rows.shape[0], down_w.shape[2]), jnp.float32)
    for half in range(2):
        gate = jnp.dot(rows, gate_w[half], preferred_element_type=jnp.float32)
        upper = jnp.dot(rows, up_w[half], preferred_element_type=jnp.float32)
        active = (jax.nn.silu(gate) * upper).astype(jnp.bfloat16)
        total = total + jnp.dot(active, down_w[half], preferred_element_type=jnp.float32)
    return total.astype(jnp.bfloat16)

def reference(queries, cache, drafts, lengths, value_up, residual, norm_gain, w_gate, w_up, w_down, routes, combine_weights):
    attended = attend(queries, cache, drafts, lengths, value_up)
    stream = residual.astype(jnp.float32) + attended
    normed = (stream * lax.rsqrt(lax.optimization_barrier(jnp.mean(stream * stream, axis=-1, keepdims=True)) + 1e-06) * norm_gain).astype(jnp.bfloat16)
    flat = routes.reshape(N_EP, TOK_DEV * TOP)
    onehot = (flat[:, :, None] == jnp.arange(EXPERTS, dtype=jnp.int32)[None, None, :]).astype(jnp.int32)
    rank = jnp.cumsum(onehot, axis=1) - onehot
    slot = lax.optimization_barrier(jnp.sum(rank * onehot, axis=-1)).astype(jnp.int32)
    rowpos = (jnp.arange(N_EP, dtype=jnp.int32)[:, None] * CAP + slot).astype(jnp.int32)
    token = (jnp.arange(N_EP, dtype=jnp.int32)[:, None] * TOK_DEV + jnp.arange(TOK_DEV * TOP, dtype=jnp.int32)[None, :] // TOP).astype(jnp.int32)
    buffer = jnp.zeros((EXPERTS, N_EP * CAP, D), jnp.bfloat16)
    buffer = buffer.at[flat.reshape(-1), rowpos.reshape(-1)].set(normed[token.reshape(-1)])
    gate_w = w_gate.reshape(EXPERTS, 2, D, FF_HALF)
    up_w = w_up.reshape(EXPERTS, 2, D, FF_HALF)
    down_w = w_down.reshape(EXPERTS, 2, FF_HALF, D)
    outputs = lax.map(run_expert, (buffer, gate_w, up_w, down_w))
    picked = outputs[flat.reshape(-1), rowpos.reshape(-1)].reshape(TOKENS, TOP, D).astype(jnp.float32)
    mixed = lax.optimization_barrier(jnp.sum(combine_weights[:, :, None] * picked, axis=1))
    return (stream + mixed).astype(jnp.bfloat16)
```

```python
import functools

import jax
import jax.numpy as jnp
from jax import lax
from jax.experimental import pallas as pl
from jax.experimental.pallas import tpu as pltpu
from jax.sharding import PartitionSpec as P

F32 = jnp.float32
BF16 = jnp.bfloat16
NT = (((1,), (1,)), ((), ()))
MIB = 1 << 20


def swapped(value, mask):
    pairs = [(source, source ^ mask) for source in range(lax.axis_size("ep"))]
    return lax.ppermute(value, "ep", pairs)


def whole():
    return pl.BlockSpec(memory_space=pltpu.VMEM)


def attend_kernel(
    heads, lengths, queries, cache, drafts, up_hbm, residual, gain, stream, normed, mixed, up, sem
):
    step = pl.program_id(0)
    rows, width = queries.shape[1:]
    slots = cache.shape[2]
    draft = drafts.shape[1]
    latent = up.shape[1]
    vdim = up.shape[2]
    copy = pltpu.make_async_copy(up_hbm, up, sem)

    @pl.when(step == 0)
    def _():
        copy.start()

    scale = (vdim + width - latent) ** (-0.5)
    q = queries[0]
    c = cache[0]
    d = drafts[0]
    cached = jnp.dot(q, c, preferred_element_type=F32) * scale
    own = lax.dot_general(q, d, NT, preferred_element_type=F32) * scale
    visible = lax.broadcasted_iota(jnp.int32, (rows, slots), 1) < lengths[step]
    token = lax.broadcasted_iota(jnp.int32, (rows, draft), 0) // heads
    causal = lax.broadcasted_iota(jnp.int32, (rows, draft), 1) <= token
    cached = jnp.where(visible, cached, -1e30)
    own = jnp.where(causal, own, -1e30)
    highest = jnp.maximum(
        jnp.max(cached, axis=-1, keepdims=True), jnp.max(own, axis=-1, keepdims=True)
    )
    e_cached = jnp.where(visible, jnp.exp(cached - highest), 0.0)
    e_own = jnp.where(causal, jnp.exp(own - highest), 0.0)
    total = jnp.sum(e_cached, axis=-1, keepdims=True) + jnp.sum(e_own, axis=-1, keepdims=True)
    inverse = 1.0 / total
    p_cached = (e_cached * inverse).astype(BF16)
    p_own = (e_own * inverse).astype(BF16)
    out = lax.dot_general(p_cached, c[:latent, :], NT, preferred_element_type=F32)
    out = out + jnp.dot(p_own, d[:, :latent], preferred_element_type=F32)
    lanes = mixed.shape[2]
    for g in range(latent // lanes):
        mixed[g, pl.ds(pl.multiple_of(step * rows, rows), rows), :] = out[
            :, g * lanes : (g + 1) * lanes
        ]

    @pl.when(step == pl.num_programs(0) - 1)
    def _():
        copy.wait()
        tokens = stream.shape[0]
        square = jnp.zeros((tokens, 1), F32)
        for head in range(heads):
            part = jnp.concatenate(
                [mixed[g, pl.ds(head, tokens, stride=heads), :] for g in range(latent // lanes)],
                axis=1,
            ).astype(BF16)
            columns = slice(head * vdim, (head + 1) * vdim)
            value = residual[:, columns].astype(F32) + jnp.dot(
                part, up[head], preferred_element_type=F32
            )
            stream[:, columns] = value
            square = square + jnp.sum(value * value, axis=-1, keepdims=True)
        factor = lax.rsqrt(square / stream.shape[1] + 1e-06)
        normed[...] = (stream[...] * factor * gain[...]).astype(BF16)


def attend(queries, cache, drafts, lengths, value_up, residual, norm_gain):
    reqs, draft, heads, width = queries.shape
    slots = cache.shape[1]
    latent, vdim = value_up.shape[1:]
    tokens, features = residual.shape
    rows = draft * heads
    flops = 2 * reqs * rows * slots * (width + latent) + 2 * tokens * heads * latent * vdim
    return pl.pallas_call(
        functools.partial(attend_kernel, heads),
        grid=(reqs,),
        in_specs=[
            pl.BlockSpec(memory_space=pltpu.SMEM),
            pl.BlockSpec((1, rows, width), lambda r: (r, 0, 0)),
            pl.BlockSpec((1, width, slots), lambda r: (r, 0, 0)),
            pl.BlockSpec((1, draft, width), lambda r: (r, 0, 0)),
            pl.BlockSpec(memory_space=pl.ANY),
            pl.BlockSpec((tokens, features), lambda r: (0, 0)),
            pl.BlockSpec((1, features), lambda r: (0, 0)),
        ],
        out_specs=[
            pl.BlockSpec((tokens, features), lambda r: (0, 0)),
            pl.BlockSpec((tokens, features), lambda r: (0, 0)),
        ],
        out_shape=[
            jax.ShapeDtypeStruct((tokens, features), F32),
            jax.ShapeDtypeStruct((tokens, features), BF16),
        ],
        scratch_shapes=[
            pltpu.VMEM((latent // 128, reqs * rows, 128), F32),
            pltpu.VMEM(value_up.shape, BF16),
            pltpu.SemaphoreType.DMA,
        ],
        cost_estimate=pl.CostEstimate(
            flops=flops, bytes_accessed=6 * MIB, transcendentals=reqs * rows * slots
        ),
        compiler_params=pltpu.CompilerParams(vmem_limit_bytes=24 * MIB),
    )(
        lengths,
        queries.reshape(reqs, rows, width),
        jnp.swapaxes(cache, 1, 2),
        drafts,
        value_up,
        residual,
        norm_gain.reshape(1, features),
    )


def table_kernel(top, tokens, stride, mine, routed, pick, high, low, table):
    experts = mine[...]
    both = routed.shape[1]
    count = experts.shape[0]
    named = jnp.zeros((count, both), F32)
    weight = jnp.zeros((count, both), F32)
    for k in range(top):
        hit = jnp.where(routed[k : k + 1, :] == experts, 1.0, 0.0)
        named = named + hit
        weight = weight + hit * routed[top + k : top + k + 1, :]
    earlier = lax.broadcasted_iota(jnp.int32, (both, both), 0)
    later = lax.broadcasted_iota(jnp.int32, (both, both), 1)
    before = (earlier < later) & ((earlier < tokens) == (later < tokens))
    rank = jnp.dot(
        named.astype(BF16),
        jnp.where(before, 1.0, 0.0).astype(BF16),
        preferred_element_type=F32,
    )
    behind = lax.broadcasted_iota(jnp.int32, (count, both), 1) >= tokens
    place = rank.astype(jnp.int32) + jnp.where(behind, stride, 0)
    place = jnp.where(named > 0.0, place, -1)
    slots = lax.broadcasted_iota(jnp.int32, (2 * stride, both), 0)
    for m in range(count):
        hit = jnp.where(slots == place[m : m + 1, :], 1.0, 0.0)
        rows = slice(2 * stride * m, 2 * stride * (m + 1))
        pick[rows, :] = hit.astype(BF16)
        table[rows, :] = hit * weight[m : m + 1, :]
    turned = table[...].T
    top_bits = turned.astype(BF16)
    high[...] = top_bits
    low[...] = (turned - top_bits.astype(F32)).astype(BF16)


def tables(mine, routed, top, tokens, stride):
    rows = mine.shape[0] * 2 * stride
    both = 2 * tokens
    return pl.pallas_call(
        functools.partial(table_kernel, top, tokens, stride),
        in_specs=[whole()] * 2,
        out_specs=[whole()] * 3,
        out_shape=[
            jax.ShapeDtypeStruct((rows, both), BF16),
            jax.ShapeDtypeStruct((both, rows), BF16),
            jax.ShapeDtypeStruct((both, rows), BF16),
        ],
        scratch_shapes=[pltpu.VMEM((rows, both), F32)],
        cost_estimate=pl.CostEstimate(flops=MIB, bytes_accessed=MIB // 4, transcendentals=0),
        compiler_params=pltpu.CompilerParams(vmem_limit_bytes=16 * MIB),
    )(mine, routed)


def dispatch_kernel(pick, here, there, *blocks):
    both = jnp.concatenate([here[...], there[...]], axis=0)
    rows = blocks[0].shape[0]
    for m, block in enumerate(blocks):
        block[...] = jnp.dot(
            pick[m * rows : (m + 1) * rows, :], both, preferred_element_type=F32
        ).astype(BF16)


def dispatch(pick, here, there, count):
    rows, width = pick.shape[0] // count, here.shape[1]
    return pl.pallas_call(
        dispatch_kernel,
        in_specs=[whole()] * 3,
        out_specs=[whole()] * count,
        out_shape=[jax.ShapeDtypeStruct((rows, width), BF16)] * count,
        cost_estimate=pl.CostEstimate(
            flops=2 * pick.size * width, bytes_accessed=3 * MIB // 2, transcendentals=0
        ),
        compiler_params=pltpu.CompilerParams(vmem_limit_bytes=16 * MIB),
    )(pick, here, there)


def expert_kernel(count, *refs):
    blocks = refs[:count]
    weights = refs[count : count + 6]
    outs = refs[count + 6 : 2 * count + 6]
    held = refs[2 * count + 6 : 2 * count + 12]
    rows_ref, total, sems = refs[2 * count + 12 :]
    copies = [pltpu.make_async_copy(weights[i], held[i], sems.at[i]) for i in range(6)]
    for copy in copies:
        copy.start()
    size = blocks[0].shape[0]
    for m, block in enumerate(blocks):
        rows_ref[m * size : (m + 1) * size, :] = block[...]
    for half in range(2):
        copies[3 * half].wait()
        gate = lax.dot_general(
            rows_ref[...], held[3 * half][...], NT, preferred_element_type=F32
        )
        copies[3 * half + 1].wait()
        upper = lax.dot_general(
            rows_ref[...], held[3 * half + 1][...], NT, preferred_element_type=F32
        )
        active = (gate * (1.0 / (1.0 + jnp.exp(-gate))) * upper).astype(BF16)
        copies[3 * half + 2].wait()
        product = jnp.dot(active, held[3 * half + 2][...], preferred_element_type=F32)
        if half == 0:
            total[...] = product
        else:
            result = (total[...] + product).astype(BF16)
            for m, out in enumerate(outs):
                out[...] = result[m * size : (m + 1) * size, :]


def run_expert(blocks, weights):
    count = len(blocks)
    size, width = blocks[0].shape
    units = weights[0].shape[0]
    return pl.pallas_call(
        functools.partial(expert_kernel, count),
        in_specs=[whole()] * count + [pl.BlockSpec(memory_space=pl.ANY)] * 6,
        out_specs=[whole()] * count,
        out_shape=[jax.ShapeDtypeStruct((size, width), BF16)] * count,
        scratch_shapes=[pltpu.VMEM((units, width), BF16)] * 6
        + [
            pltpu.VMEM((count * size, width), BF16),
            pltpu.VMEM((count * size, width), F32),
            pltpu.SemaphoreType.DMA((6,)),
        ],
        cost_estimate=pl.CostEstimate(
            flops=12 * count * size * width * units,
            bytes_accessed=12 * units * width,
            transcendentals=2 * count * size * units,
        ),
        compiler_params=pltpu.CompilerParams(vmem_limit_bytes=48 * MIB),
    )(*blocks, *weights)


def combine_kernel(high, low, *refs):
    blocks, (here, there) = refs[:-2], refs[-2:]
    rows = jnp.concatenate([block[...] for block in blocks], axis=0)
    total = jnp.dot(high[...], rows, preferred_element_type=F32)
    total = total + jnp.dot(low[...], rows, preferred_element_type=F32)
    tokens = here.shape[0]
    here[...] = total[:tokens]
    there[...] = total[tokens:].astype(BF16)


def combine(high, low, blocks):
    both, rows = high.shape
    width = blocks[0].shape[1]
    return pl.pallas_call(
        combine_kernel,
        in_specs=[whole()] * (2 + len(blocks)),
        out_specs=[whole()] * 2,
        out_shape=[
            jax.ShapeDtypeStruct((both // 2, width), F32),
            jax.ShapeDtypeStruct((both // 2, width), BF16),
        ],
        cost_estimate=pl.CostEstimate(
            flops=4 * both * rows * width, bytes_accessed=3 * MIB // 2, transcendentals=0
        ),
        compiler_params=pltpu.CompilerParams(vmem_limit_bytes=16 * MIB),
    )(high, low, *blocks)


def local(
    queries,
    cache,
    drafts,
    lengths,
    value_up,
    residual,
    norm_gain,
    w_gate,
    w_up,
    w_down,
    routes,
    combine_weights,
):
    tokens, top = routes.shape
    devices = lax.axis_size("ep")
    experts = devices // 2
    near = experts // 2
    capacity = min(tokens, 2 * (((tokens * top + experts - 1) // experts + 3) // 2))
    stride = -(-capacity // 8) * 8

    routed = jnp.concatenate([routes.T.astype(F32), combine_weights.T], axis=0)
    routed = jnp.concatenate([routed, swapped(routed, devices // 2)], axis=1)
    own = [jnp.swapaxes(w_gate, 1, 2)[0], jnp.swapaxes(w_up, 1, 2)[0], w_down[0]]
    weights = own + [swapped(w, 1) for w in own]
    chip = lax.axis_index("ep") // 2
    mine = (chip ^ jnp.arange(near, dtype=jnp.int32)).astype(F32)[:, None]

    stream, normed = attend(queries, cache, drafts, lengths, value_up, residual, norm_gain)
    pick, high, low = tables(mine, routed, top, tokens, stride)
    blocks = dispatch(pick, normed, swapped(normed, devices // 2), near)
    blocks = [swapped(b, 2 * m) if m else b for m, b in enumerate(blocks)]
    blocks = run_expert(blocks, weights)
    blocks = [swapped(b, 2 * m) if m else b for m, b in enumerate(blocks)]
    here, there = combine(high, low, blocks)
    return (stream + (here + swapped(there, devices // 2).astype(F32))).astype(BF16)


def solution(mesh):
    placed = (
        P(("groups", "ep"), None, None, None),
        P(("groups", "ep"), None, None),
        P(("groups", "ep"), None, None),
        P(("groups", "ep")),
        P(),
        P(("groups", "ep"), None),
        P(),
        P("ep", None, None),
        P("ep", None, None),
        P("ep", None, None),
        P(("groups", "ep"), None),
        P(("groups", "ep"), None),
    )
    return jax.shard_map(
        local, mesh=mesh, in_specs=placed, out_specs=P(("groups", "ep"), None), check_vma=False
    )
```

```python
import functools

import jax
import jax.numpy as jnp
from jax import lax
from jax.experimental import pallas as pl
from jax.experimental.pallas import tpu as pltpu
from jax.sharding import PartitionSpec as P

F32 = jnp.float32
BF16 = jnp.bfloat16
NT = (((1,), (1,)), ((), ()))
MIB = 1 << 20


def swapped(value, mask):
    pairs = [(source, source ^ mask) for source in range(lax.axis_size("ep"))]
    return lax.ppermute(value, "ep", pairs)


def whole():
    return pl.BlockSpec(memory_space=pltpu.VMEM)


def attend_kernel(heads, *refs):
    given, (stream, normed), held = refs[:7], refs[7:9], refs[9:16]
    mixed, sems = refs[16:]
    lengths, queries, cache, drafts, up, residual, gain = held
    reqs, rows, width = queries.shape
    parts = [(0, None), (3, None)]
    parts += [(i, r) for r in range(reqs) for i in (1, 2)]
    parts += [(4, None), (5, None), (6, None)]
    copies = {}
    for n, (i, r) in enumerate(parts):
        source, target = (given[i], held[i]) if r is None else (given[i].at[r], held[i].at[r])
        copies[i, r] = pltpu.make_async_copy(source, target, sems.at[n])
        copies[i, r].start()
    slots = cache.shape[2]
    draft = drafts.shape[1]
    latent, vdim = up.shape[1:]
    lanes = mixed.shape[2]
    scale = (vdim + width - latent) ** (-0.5)
    position = lax.broadcasted_iota(jnp.int32, (rows, slots), 1)
    token = lax.broadcasted_iota(jnp.int32, (rows, draft), 0) // heads
    causal = lax.broadcasted_iota(jnp.int32, (rows, draft), 1) <= token
    copies[0, None].wait()
    copies[3, None].wait()
    for r in range(reqs):
        copies[1, r].wait()
        copies[2, r].wait()
        q, c, d = queries[r], cache[r], drafts[r]
        cached = jnp.dot(q, c, preferred_element_type=F32) * scale
        own = lax.dot_general(q, d, NT, preferred_element_type=F32) * scale
        visible = position < lengths[r]
        cached = jnp.where(visible, cached, -1e30)
        own = jnp.where(causal, own, -1e30)
        highest = jnp.maximum(
            jnp.max(cached, axis=-1, keepdims=True), jnp.max(own, axis=-1, keepdims=True)
        )
        e_cached = jnp.where(visible, jnp.exp(cached - highest), 0.0)
        e_own = jnp.where(causal, jnp.exp(own - highest), 0.0)
        total = jnp.sum(e_cached, axis=-1, keepdims=True) + jnp.sum(e_own, axis=-1, keepdims=True)
        inverse = 1.0 / total
        p_cached = (e_cached * inverse).astype(BF16)
        p_own = (e_own * inverse).astype(BF16)
        out = lax.dot_general(p_cached, c[:latent, :], NT, preferred_element_type=F32)
        out = out + jnp.dot(p_own, d[:, :latent], preferred_element_type=F32)
        for g in range(latent // lanes):
            mixed[g, r * rows : (r + 1) * rows, :] = out[:, g * lanes : (g + 1) * lanes]
    for i in (4, 5, 6):
        copies[i, None].wait()
    tokens = stream.shape[0]
    square = jnp.zeros((tokens, 1), F32)
    for head in range(heads):
        part = jnp.concatenate(
            [mixed[g, pl.ds(head, tokens, stride=heads), :] for g in range(latent // lanes)],
            axis=1,
        ).astype(BF16)
        columns = slice(head * vdim, (head + 1) * vdim)
        value = residual[:, columns].astype(F32) + jnp.dot(
            part, up[head], preferred_element_type=F32
        )
        stream[:, columns] = value
        square = square + jnp.sum(value * value, axis=-1, keepdims=True)
    factor = lax.rsqrt(square / stream.shape[1] + 1e-06)
    normed[...] = (stream[...] * factor * gain[...]).astype(BF16)


def attend(queries, cache, drafts, lengths, value_up, residual, norm_gain):
    reqs, draft, heads, width = queries.shape
    slots = cache.shape[1]
    latent, vdim = value_up.shape[1:]
    tokens, features = residual.shape
    rows = draft * heads
    flops = 2 * reqs * rows * slots * (width + latent) + 2 * tokens * heads * latent * vdim
    operands = (
        lengths,
        queries.reshape(reqs, rows, width),
        jnp.swapaxes(cache, 1, 2),
        drafts,
        value_up,
        residual,
        norm_gain.reshape(1, features),
    )
    return pl.pallas_call(
        functools.partial(attend_kernel, heads),
        in_specs=[pl.BlockSpec(memory_space=pltpu.HBM)] * 7,
        out_specs=[whole()] * 2,
        out_shape=[
            jax.ShapeDtypeStruct((tokens, features), F32),
            jax.ShapeDtypeStruct((tokens, features), BF16),
        ],
        scratch_shapes=[pltpu.SMEM(lengths.shape, jnp.int32)]
        + [pltpu.VMEM(o.shape, o.dtype) for o in operands[1:]]
        + [
            pltpu.VMEM((latent // 128, reqs * rows, 128), F32),
            pltpu.SemaphoreType.DMA((2 * reqs + 5,)),
        ],
        cost_estimate=pl.CostEstimate(
            flops=flops, bytes_accessed=6 * MIB, transcendentals=reqs * rows * slots
        ),
        compiler_params=pltpu.CompilerParams(vmem_limit_bytes=60 * MIB),
    )(*operands)


def table_kernel(top, tokens, stride, mine, routed, pick, high, low, table):
    experts = mine[...]
    both = routed.shape[1]
    count = experts.shape[0]
    named = jnp.zeros((count, both), F32)
    weight = jnp.zeros((count, both), F32)
    for k in range(top):
        hit = jnp.where(routed[k : k + 1, :] == experts, 1.0, 0.0)
        named = named + hit
        weight = weight + hit * routed[top + k : top + k + 1, :]
    earlier = lax.broadcasted_iota(jnp.int32, (both, both), 0)
    later = lax.broadcasted_iota(jnp.int32, (both, both), 1)
    before = (earlier < later) & ((earlier < tokens) == (later < tokens))
    rank = jnp.dot(
        named.astype(BF16),
        jnp.where(before, 1.0, 0.0).astype(BF16),
        preferred_element_type=F32,
    )
    behind = lax.broadcasted_iota(jnp.int32, (count, both), 1) >= tokens
    place = rank.astype(jnp.int32) + jnp.where(behind, stride, 0)
    place = jnp.where(named > 0.0, place, -1)
    slots = lax.broadcasted_iota(jnp.int32, (2 * stride, both), 0)
    for m in range(count):
        hit = jnp.where(slots == place[m : m + 1, :], 1.0, 0.0)
        rows = slice(2 * stride * m, 2 * stride * (m + 1))
        pick[rows, :] = hit.astype(BF16)
        table[rows, :] = hit * weight[m : m + 1, :]
    turned = table[...].T
    top_bits = turned.astype(BF16)
    high[...] = top_bits
    low[...] = (turned - top_bits.astype(F32)).astype(BF16)


def tables(mine, routed, top, tokens, stride):
    rows = mine.shape[0] * 2 * stride
    both = 2 * tokens
    return pl.pallas_call(
        functools.partial(table_kernel, top, tokens, stride),
        in_specs=[whole()] * 2,
        out_specs=[whole()] * 3,
        out_shape=[
            jax.ShapeDtypeStruct((rows, both), BF16),
            jax.ShapeDtypeStruct((both, rows), BF16),
            jax.ShapeDtypeStruct((both, rows), BF16),
        ],
        scratch_shapes=[pltpu.VMEM((rows, both), F32)],
        cost_estimate=pl.CostEstimate(flops=MIB, bytes_accessed=MIB // 4, transcendentals=0),
        compiler_params=pltpu.CompilerParams(vmem_limit_bytes=16 * MIB),
    )(mine, routed)


def dispatch_kernel(pick, here, there, *blocks):
    both = jnp.concatenate([here[...], there[...]], axis=0)
    rows = blocks[0].shape[0]
    for m, block in enumerate(blocks):
        block[...] = jnp.dot(
            pick[m * rows : (m + 1) * rows, :], both, preferred_element_type=F32
        ).astype(BF16)


def dispatch(pick, here, there, count):
    rows, width = pick.shape[0] // count, here.shape[1]
    return pl.pallas_call(
        dispatch_kernel,
        in_specs=[whole()] * 3,
        out_specs=[whole()] * count,
        out_shape=[jax.ShapeDtypeStruct((rows, width), BF16)] * count,
        cost_estimate=pl.CostEstimate(
            flops=2 * pick.size * width, bytes_accessed=3 * MIB // 2, transcendentals=0
        ),
        compiler_params=pltpu.CompilerParams(vmem_limit_bytes=16 * MIB),
    )(pick, here, there)


def load_kernel(*refs):
    count = len(refs) // 2
    sems = refs[-1]
    copies = [
        pltpu.make_async_copy(refs[i], refs[count + i], sems.at[i]) for i in range(count)
    ]
    for copy in copies:
        copy.start()
    for copy in copies:
        copy.wait()


def load(weights, room):
    return pl.pallas_call(
        load_kernel,
        in_specs=[pl.BlockSpec(memory_space=pl.ANY)] * len(weights),
        out_specs=[whole()] * len(weights),
        out_shape=[jax.ShapeDtypeStruct(w.shape, w.dtype) for w in weights],
        scratch_shapes=[pltpu.SemaphoreType.DMA((len(weights),))],
        cost_estimate=pl.CostEstimate(
            flops=0, bytes_accessed=2 * sum(2 * w.size for w in weights), transcendentals=0
        ),
        compiler_params=pltpu.CompilerParams(vmem_limit_bytes=room * MIB),
    )(*weights)


def expert_kernel(count, *refs):
    blocks = refs[:count]
    near, far = refs[count : count + 3], refs[count + 3 : count + 6]
    outs = refs[count + 6 : 2 * count + 6]
    held = refs[2 * count + 6 : 2 * count + 9]
    rows_ref, total, sems = refs[2 * count + 9 :]
    copies = [pltpu.make_async_copy(far[i], held[i], sems.at[i]) for i in range(3)]
    for copy in copies:
        copy.start()
    size = blocks[0].shape[0]
    for m, block in enumerate(blocks):
        rows_ref[m * size : (m + 1) * size, :] = block[...]

    def half(weights, ready):
        w_gate, w_up, w_down = weights
        ready(0)
        gate = lax.dot_general(rows_ref[...], w_gate[...], NT, preferred_element_type=F32)
        ready(1)
        upper = lax.dot_general(rows_ref[...], w_up[...], NT, preferred_element_type=F32)
        active = (gate * (1.0 / (1.0 + jnp.exp(-gate))) * upper).astype(BF16)
        ready(2)
        return jnp.dot(active, w_down[...], preferred_element_type=F32)

    total[...] = half(near, lambda i: None)
    result = (total[...] + half(held, lambda i: copies[i].wait())).astype(BF16)
    for m, out in enumerate(outs):
        out[...] = result[m * size : (m + 1) * size, :]


def run_expert(blocks, near, far):
    count = len(blocks)
    size, width = blocks[0].shape
    units = near[0].shape[0]
    return pl.pallas_call(
        functools.partial(expert_kernel, count),
        in_specs=[whole()] * (count + 3) + [pl.BlockSpec(memory_space=pl.ANY)] * 3,
        out_specs=[whole()] * count,
        out_shape=[jax.ShapeDtypeStruct((size, width), BF16)] * count,
        scratch_shapes=[pltpu.VMEM((units, width), BF16)] * 3
        + [
            pltpu.VMEM((count * size, width), BF16),
            pltpu.VMEM((count * size, width), F32),
            pltpu.SemaphoreType.DMA((3,)),
        ],
        cost_estimate=pl.CostEstimate(
            flops=12 * count * size * width * units,
            bytes_accessed=12 * units * width,
            transcendentals=2 * count * size * units,
        ),
        compiler_params=pltpu.CompilerParams(vmem_limit_bytes=36 * MIB),
    )(*blocks, *near, *far)


def combine_kernel(high, low, *refs):
    blocks, (here, there) = refs[:-2], refs[-2:]
    rows = jnp.concatenate([block[...] for block in blocks], axis=0)
    total = jnp.dot(high[...], rows, preferred_element_type=F32)
    total = total + jnp.dot(low[...], rows, preferred_element_type=F32)
    tokens = here.shape[0]
    here[...] = total[:tokens]
    there[...] = total[tokens:].astype(BF16)


def combine(high, low, blocks):
    both, rows = high.shape
    width = blocks[0].shape[1]
    return pl.pallas_call(
        combine_kernel,
        in_specs=[whole()] * (2 + len(blocks)),
        out_specs=[whole()] * 2,
        out_shape=[
            jax.ShapeDtypeStruct((both // 2, width), F32),
            jax.ShapeDtypeStruct((both // 2, width), BF16),
        ],
        cost_estimate=pl.CostEstimate(
            flops=4 * both * rows * width, bytes_accessed=3 * MIB // 2, transcendentals=0
        ),
        compiler_params=pltpu.CompilerParams(vmem_limit_bytes=16 * MIB),
    )(high, low, *blocks)


def local(
    queries,
    cache,
    drafts,
    lengths,
    value_up,
    residual,
    norm_gain,
    w_gate,
    w_up,
    w_down,
    routes,
    combine_weights,
):
    tokens, top = routes.shape
    devices = lax.axis_size("ep")
    experts = devices // 2
    near = experts // 2
    capacity = min(tokens, 2 * (((tokens * top + experts - 1) // experts + 3) // 2))
    stride = -(-capacity // 8) * 8

    routed = jnp.concatenate([routes.T.astype(F32), combine_weights.T], axis=0)
    own = [jnp.swapaxes(w_gate, 1, 2)[0], jnp.swapaxes(w_up, 1, 2)[0], w_down[0]]
    other = [swapped(w, 1) for w in own]
    chip = lax.axis_index("ep") // 2
    mine = (chip ^ jnp.arange(near, dtype=jnp.int32)).astype(F32)[:, None]

    stream, normed = attend(queries, cache, drafts, lengths, value_up, residual, norm_gain)
    routed, normed, own = lax.optimization_barrier((routed, normed, own))
    across = swapped(normed, devices // 2)
    routed = jnp.concatenate([routed, swapped(routed, devices // 2)], axis=1)
    pick, high, low = tables(mine, routed, top, tokens, stride)
    own = load(own, 44)
    across, own, other = lax.optimization_barrier((across, own, other))
    blocks = dispatch(pick, normed, across, near)
    blocks = [swapped(b, 2 * m) if m else b for m, b in enumerate(blocks)]
    blocks = run_expert(blocks, own, other)
    blocks = [swapped(b, 2 * m) if m else b for m, b in enumerate(blocks)]
    here, there = combine(high, low, blocks)
    return (stream + (here + swapped(there, devices // 2).astype(F32))).astype(BF16)


def solution(mesh):
    placed = (
        P(("groups", "ep"), None, None, None),
        P(("groups", "ep"), None, None),
        P(("groups", "ep"), None, None),
        P(("groups", "ep")),
        P(),
        P(("groups", "ep"), None),
        P(),
        P("ep", None, None),
        P("ep", None, None),
        P("ep", None, None),
        P(("groups", "ep"), None),
        P(("groups", "ep"), None),
    )
    return jax.shard_map(
        local, mesh=mesh, in_specs=placed, out_specs=P(("groups", "ep"), None), check_vma=False
    )
```

```python
import functools

import jax
import jax.numpy as jnp
from jax import lax
from jax.experimental import pallas as pl
from jax.experimental.pallas import tpu as pltpu
from jax.sharding import PartitionSpec as P

F32 = jnp.float32
BF16 = jnp.bfloat16
NT = (((1,), (1,)), ((), ()))
MIB = 1 << 20


def swapped(value, mask):
    pairs = [(source, source ^ mask) for source in range(lax.axis_size("ep"))]
    return lax.ppermute(value, "ep", pairs)


def exchanged(blocks):
    last = len(blocks) - 1
    return [swapped(b, 2 * (last - i)) if i < last else b for i, b in enumerate(blocks)]


def whole():
    return pl.BlockSpec(memory_space=pltpu.VMEM)


def attend_kernel(heads, *refs):
    given, (routes, shares), (stream, normed) = refs[:7], refs[7:9], refs[9:11]
    held, (mixed, sems) = refs[11:18], refs[18:]
    lengths, queries, cache, drafts, up, residual, gain = held
    reqs, rows, width = queries.shape
    parts = [(0, None), (3, None)]
    parts += [(i, r) for r in range(reqs) for i in (1, 2)]
    parts += [(4, None), (5, None), (6, None)]
    copies = {}
    for n, (i, r) in enumerate(parts):
        source, target = (given[i], held[i]) if r is None else (given[i].at[r], held[i].at[r])
        copies[i, r] = pltpu.make_async_copy(source, target, sems.at[n])
        copies[i, r].start()
    slots = cache.shape[2]
    draft = drafts.shape[1]
    latent, vdim = up.shape[1:]
    lanes = mixed.shape[2]
    scale = (vdim + width - latent) ** (-0.5)
    position = lax.broadcasted_iota(jnp.int32, (rows, slots), 1)
    token = lax.broadcasted_iota(jnp.int32, (rows, draft), 0) // heads
    causal = lax.broadcasted_iota(jnp.int32, (rows, draft), 1) <= token
    copies[0, None].wait()
    copies[3, None].wait()
    for r in range(reqs):
        copies[1, r].wait()
        copies[2, r].wait()
        q, c, d = queries[r], cache[r], drafts[r]
        cached = jnp.dot(q, c, preferred_element_type=F32) * scale
        own = lax.dot_general(q, d, NT, preferred_element_type=F32) * scale
        visible = position < lengths[r]
        cached = jnp.where(visible, cached, -1e30)
        own = jnp.where(causal, own, -1e30)
        highest = jnp.maximum(
            jnp.max(cached, axis=-1, keepdims=True), jnp.max(own, axis=-1, keepdims=True)
        )
        e_cached = jnp.where(visible, jnp.exp(cached - highest), 0.0)
        e_own = jnp.where(causal, jnp.exp(own - highest), 0.0)
        total = jnp.sum(e_cached, axis=-1, keepdims=True) + jnp.sum(e_own, axis=-1, keepdims=True)
        inverse = 1.0 / total
        p_cached = (e_cached * inverse).astype(BF16)
        p_own = (e_own * inverse).astype(BF16)
        out = lax.dot_general(p_cached, c[:latent, :], NT, preferred_element_type=F32)
        out = out + jnp.dot(p_own, d[:, :latent], preferred_element_type=F32)
        for g in range(latent // lanes):
            mixed[g, r * rows : (r + 1) * rows, :] = out[:, g * lanes : (g + 1) * lanes]
    for i in (4, 5, 6):
        copies[i, None].wait()
    tokens = stream.shape[0]
    square = jnp.zeros((tokens, 1), F32)
    for head in range(heads):
        part = jnp.concatenate(
            [mixed[g, pl.ds(head, tokens, stride=heads), :] for g in range(latent // lanes)],
            axis=1,
        ).astype(BF16)
        columns = slice(head * vdim, (head + 1) * vdim)
        value = residual[:, columns].astype(F32) + jnp.dot(
            part, up[head], preferred_element_type=F32
        )
        stream[:, columns] = value
        square = square + jnp.sum(value * value, axis=-1, keepdims=True)
    factor = lax.rsqrt(square / stream.shape[1] + 1e-06)
    features = stream.shape[1]
    normed[:, :features] = (stream[...] * factor * gain[...]).astype(BF16)
    normed[:, features:] = packed(routes[...], shares[...], tokens)


def packed(routes, shares, tokens):
    top = routes.shape[0]
    first = shares.astype(BF16).astype(F32)
    second = (shares - first).astype(BF16).astype(F32)
    third = shares - first - second
    rows = jnp.concatenate([routes.astype(F32), first, second, third], axis=1)
    rest = jnp.zeros((tokens - top, rows.shape[1]), F32)
    return jnp.concatenate([rows, rest], axis=0).astype(BF16)


def unpacked(block, top, tokens):
    rows = block[...].astype(F32)[:top]
    parts = [rows[:, i * tokens : (i + 1) * tokens] for i in range(4)]
    return parts[0], parts[1] + parts[2] + parts[3]


def attend(queries, cache, drafts, lengths, value_up, residual, norm_gain, routes, shares):
    reqs, draft, heads, width = queries.shape
    slots = cache.shape[1]
    latent, vdim = value_up.shape[1:]
    tokens, features = residual.shape
    rows = draft * heads
    flops = 2 * reqs * rows * slots * (width + latent) + 2 * tokens * heads * latent * vdim
    operands = (
        lengths,
        queries.reshape(reqs, rows, width),
        jnp.swapaxes(cache, 1, 2),
        drafts,
        value_up,
        residual,
        norm_gain.reshape(1, features),
    )
    return pl.pallas_call(
        functools.partial(attend_kernel, heads),
        in_specs=[pl.BlockSpec(memory_space=pltpu.HBM)] * 7 + [whole()] * 2,
        out_specs=[whole()] * 2,
        out_shape=[
            jax.ShapeDtypeStruct((tokens, features), F32),
            jax.ShapeDtypeStruct((tokens, features + 4 * tokens), BF16),
        ],
        scratch_shapes=[pltpu.SMEM(lengths.shape, jnp.int32)]
        + [pltpu.VMEM(o.shape, o.dtype) for o in operands[1:]]
        + [
            pltpu.VMEM((latent // 128, reqs * rows, 128), F32),
            pltpu.SemaphoreType.DMA((2 * reqs + 5,)),
        ],
        cost_estimate=pl.CostEstimate(
            flops=flops, bytes_accessed=6 * MIB, transcendentals=reqs * rows * slots
        ),
        compiler_params=pltpu.CompilerParams(vmem_limit_bytes=60 * MIB),
    )(*operands, routes, shares)


def dispatch_kernel(top, stride, mine, here, there, high, low, *refs):
    blocks, table = refs[:-1], refs[-1]
    tokens, features = here.shape[0], blocks[0].shape[1]
    here_routes, here_shares = unpacked(here.at[:, features:], top, tokens)
    there_routes, there_shares = unpacked(there.at[:, features:], top, tokens)
    routes = jnp.concatenate([here_routes, there_routes], axis=1)
    shares = jnp.concatenate([here_shares, there_shares], axis=1)
    experts = mine[...]
    both = 2 * tokens
    count = experts.shape[0]
    named = jnp.zeros((count, both), F32)
    weight = jnp.zeros((count, both), F32)
    for k in range(top):
        hit = jnp.where(routes[k : k + 1, :] == experts, 1.0, 0.0)
        named = named + hit
        weight = weight + hit * shares[k : k + 1, :]
    earlier = lax.broadcasted_iota(jnp.int32, (both, both), 0)
    later = lax.broadcasted_iota(jnp.int32, (both, both), 1)
    before = (earlier < later) & ((earlier < tokens) == (later < tokens))
    rank = jnp.dot(
        named.astype(BF16),
        jnp.where(before, 1.0, 0.0).astype(BF16),
        preferred_element_type=F32,
    )
    behind = lax.broadcasted_iota(jnp.int32, (count, both), 1) >= tokens
    place = rank.astype(jnp.int32) + jnp.where(behind, stride, 0)
    place = jnp.where(named > 0.0, place, -1)
    slots = lax.broadcasted_iota(jnp.int32, (2 * stride, both), 0)
    rows = jnp.concatenate([here[:, :features], there[:, :features]], axis=0)
    for m, block in enumerate(blocks):
        hit = jnp.where(slots == place[m : m + 1, :], 1.0, 0.0)
        table[2 * stride * m : 2 * stride * (m + 1), :] = hit * weight[m : m + 1, :]
        block[...] = jnp.dot(hit.astype(BF16), rows, preferred_element_type=F32).astype(BF16)
    turned = table[...].T
    top_bits = turned.astype(BF16)
    high[...] = top_bits
    low[...] = (turned - top_bits.astype(F32)).astype(BF16)


def dispatch(mine, here, there, top, stride):
    count, both = mine.shape[0], 2 * here.shape[0]
    width = here.shape[1] - 2 * both
    rows = count * 2 * stride
    return pl.pallas_call(
        functools.partial(dispatch_kernel, top, stride),
        in_specs=[whole()] * 3,
        out_specs=[whole()] * (2 + count),
        out_shape=[jax.ShapeDtypeStruct((both, rows), BF16)] * 2
        + [jax.ShapeDtypeStruct((2 * stride, width), BF16)] * count,
        scratch_shapes=[pltpu.VMEM((rows, both), F32)],
        cost_estimate=pl.CostEstimate(
            flops=2 * rows * both * width, bytes_accessed=3 * MIB // 2, transcendentals=0
        ),
        compiler_params=pltpu.CompilerParams(vmem_limit_bytes=16 * MIB),
    )(mine, here, there)


def load_kernel(*refs):
    count = len(refs) // 2
    sems = refs[-1]
    copies = [
        pltpu.make_async_copy(refs[i], refs[count + i], sems.at[i]) for i in range(count)
    ]
    for copy in copies:
        copy.start()
    for copy in copies:
        copy.wait()


def load(weights, room):
    return pl.pallas_call(
        load_kernel,
        in_specs=[pl.BlockSpec(memory_space=pl.ANY)] * len(weights),
        out_specs=[whole()] * len(weights),
        out_shape=[jax.ShapeDtypeStruct(w.shape, w.dtype) for w in weights],
        scratch_shapes=[pltpu.SemaphoreType.DMA((len(weights),))],
        cost_estimate=pl.CostEstimate(
            flops=0, bytes_accessed=2 * sum(2 * w.size for w in weights), transcendentals=0
        ),
        compiler_params=pltpu.CompilerParams(vmem_limit_bytes=room * MIB),
    )(*weights)


def expert_kernel(count, *refs):
    blocks = refs[:count]
    near, far = refs[count : count + 3], refs[count + 3 : count + 6]
    outs = refs[count + 6 : 2 * count + 6]
    held = refs[2 * count + 6 : 2 * count + 9]
    rows_ref, total, sems = refs[2 * count + 9 :]
    copies = [pltpu.make_async_copy(far[i], held[i], sems.at[i]) for i in range(3)]
    for copy in copies:
        copy.start()
    size = blocks[0].shape[0]
    for m, block in enumerate(blocks):
        rows_ref[m * size : (m + 1) * size, :] = block[...]

    def half(weights, ready):
        w_gate, w_up, w_down = weights
        ready(0)
        gate = lax.dot_general(rows_ref[...], w_gate[...], NT, preferred_element_type=F32)
        ready(1)
        upper = lax.dot_general(rows_ref[...], w_up[...], NT, preferred_element_type=F32)
        active = (gate * (1.0 / (1.0 + jnp.exp(-gate))) * upper).astype(BF16)
        ready(2)
        return jnp.dot(active, w_down[...], preferred_element_type=F32)

    total[...] = half(near, lambda i: None)
    result = (total[...] + half(held, lambda i: copies[i].wait())).astype(BF16)
    for m, out in enumerate(outs):
        out[...] = result[m * size : (m + 1) * size, :]


def run_expert(blocks, near, far):
    count = len(blocks)
    size, width = blocks[0].shape
    units = near[0].shape[0]
    return pl.pallas_call(
        functools.partial(expert_kernel, count),
        in_specs=[whole()] * (count + 3) + [pl.BlockSpec(memory_space=pl.ANY)] * 3,
        out_specs=[whole()] * count,
        out_shape=[jax.ShapeDtypeStruct((size, width), BF16)] * count,
        scratch_shapes=[pltpu.VMEM((units, width), BF16)] * 3
        + [
            pltpu.VMEM((count * size, width), BF16),
            pltpu.VMEM((count * size, width), F32),
            pltpu.SemaphoreType.DMA((3,)),
        ],
        cost_estimate=pl.CostEstimate(
            flops=12 * count * size * width * units,
            bytes_accessed=12 * units * width,
            transcendentals=2 * count * size * units,
        ),
        compiler_params=pltpu.CompilerParams(vmem_limit_bytes=36 * MIB),
    )(*blocks, *near, *far)


def combine_kernel(high, low, *refs):
    blocks, (here, there) = refs[:-2], refs[-2:]
    rows = jnp.concatenate([block[...] for block in blocks], axis=0)
    total = jnp.dot(high[...], rows, preferred_element_type=F32)
    total = total + jnp.dot(low[...], rows, preferred_element_type=F32)
    tokens = here.shape[0]
    here[...] = total[:tokens]
    there[...] = total[tokens:].astype(BF16)


def combine(high, low, blocks):
    both, rows = high.shape
    width = blocks[0].shape[1]
    return pl.pallas_call(
        combine_kernel,
        in_specs=[whole()] * (2 + len(blocks)),
        out_specs=[whole()] * 2,
        out_shape=[
            jax.ShapeDtypeStruct((both // 2, width), F32),
            jax.ShapeDtypeStruct((both // 2, width), BF16),
        ],
        cost_estimate=pl.CostEstimate(
            flops=4 * both * rows * width, bytes_accessed=3 * MIB // 2, transcendentals=0
        ),
        compiler_params=pltpu.CompilerParams(vmem_limit_bytes=16 * MIB),
    )(high, low, *blocks)


def local(
    queries,
    cache,
    drafts,
    lengths,
    value_up,
    residual,
    norm_gain,
    w_gate,
    w_up,
    w_down,
    routes,
    combine_weights,
):
    tokens, top = routes.shape
    devices = lax.axis_size("ep")
    experts = devices // 2
    near = experts // 2
    capacity = min(tokens, 2 * (((tokens * top + experts - 1) // experts + 3) // 2))
    stride = -(-capacity // 8) * 8

    own = [jnp.swapaxes(w_gate, 1, 2)[0], jnp.swapaxes(w_up, 1, 2)[0], w_down[0]]
    other = [swapped(w, 1) for w in own]
    chip = lax.axis_index("ep") // 2
    mine = (chip ^ jnp.arange(near - 1, -1, -1, dtype=jnp.int32)).astype(F32)[:, None]

    stream, normed = attend(
        queries, cache, drafts, lengths, value_up, residual, norm_gain, routes.T, combine_weights.T
    )
    normed, own = lax.optimization_barrier((normed, own))
    across = swapped(normed, devices // 2)
    own = load(own, 44)
    across, own, other = lax.optimization_barrier((across, own, other))
    high, low, *blocks = dispatch(mine, normed, across, top, stride)
    blocks = exchanged(blocks)
    blocks = exchanged(run_expert(blocks, own, other))
    here, there = combine(high, low, blocks)
    return (stream + (here + swapped(there, devices // 2).astype(F32))).astype(BF16)


def solution(mesh):
    placed = (
        P(("groups", "ep"), None, None, None),
        P(("groups", "ep"), None, None),
        P(("groups", "ep"), None, None),
        P(("groups", "ep")),
        P(),
        P(("groups", "ep"), None),
        P(),
        P("ep", None, None),
        P("ep", None, None),
        P("ep", None, None),
        P(("groups", "ep"), None),
        P(("groups", "ep"), None),
    )
    return jax.shard_map(
        local, mesh=mesh, in_specs=placed, out_specs=P(("groups", "ep"), None), check_vma=False
    )
```

```python
import functools

import jax
import jax.numpy as jnp
from jax import lax
from jax.experimental import pallas as pl
from jax.experimental.pallas import tpu as pltpu
from jax.sharding import PartitionSpec as P

F32 = jnp.float32
BF16 = jnp.bfloat16
NT = (((1,), (1,)), ((), ()))
MIB = 1 << 20


def swapped(value, mask):
    pairs = [(source, source ^ mask) for source in range(lax.axis_size("ep"))]
    return lax.ppermute(value, "ep", pairs)


def exchanged(blocks):
    last = len(blocks) - 1
    return [swapped(b, 2 * (last - i)) if i < last else b for i, b in enumerate(blocks)]


def whole():
    return pl.BlockSpec(memory_space=pltpu.VMEM)


def attend_kernel(heads, *refs):
    given, (stream, normed), held = refs[:9], refs[9:11], refs[11:20]
    mixed, sems = refs[20:]
    lengths, drafts, queries, cache, up, residual, gain, routes, shares = held
    reqs, rows, width = queries.shape
    slots = given[3].shape[2]
    draft = drafts.shape[1]
    latent, vdim = up.shape[1:]
    lanes = mixed.shape[2]
    columns = cache.shape[2]
    copies = {}
    order = [(0, None), (1, None)] + [(i, r) for r in range(reqs) for i in (2, 3)]
    for n, (i, r) in enumerate(order + [(i, None) for i in range(4, 9)]):
        source, target = (given[i], held[i]) if r is None else (given[i].at[r], held[i].at[r])
        if i == 3:
            target = target.at[:, :slots]
        copies[i, r] = pltpu.make_async_copy(source, target, sems.at[n])
        copies[i, r].start()
    scale = (vdim + width - latent) ** (-0.5)
    place = lax.broadcasted_iota(jnp.int32, (rows, columns), 1)
    token = lax.broadcasted_iota(jnp.int32, (rows, columns), 0) // heads
    causal = (place >= slots) & (place - slots <= token)
    copies[0, None].wait()
    copies[1, None].wait()
    for r in range(reqs):
        d = jnp.concatenate(
            [drafts[r].astype(F32), jnp.zeros((columns - slots - draft, width), F32)], axis=0
        )
        cache[r, :, slots:] = d.T.astype(BF16)
    for r in range(reqs):
        copies[2, r].wait()
        copies[3, r].wait()
        score = jnp.dot(queries[r], cache[r], preferred_element_type=F32) * scale
        score = jnp.where((place < lengths[r]) | causal, score, -1e30)
        e = jnp.exp(score - jnp.max(score, axis=-1, keepdims=True))
        p = (e * (1.0 / jnp.sum(e, axis=-1, keepdims=True))).astype(BF16)
        out = lax.dot_general(p, cache[r, :latent, :], NT, preferred_element_type=F32)
        for g in range(latent // lanes):
            mixed[g, r * rows : (r + 1) * rows, :] = out[:, g * lanes : (g + 1) * lanes]
    for i in range(4, 9):
        copies[i, None].wait()
    tokens, features = stream.shape
    square = jnp.zeros((tokens, 1), F32)
    for head in range(heads):
        part = jnp.concatenate(
            [mixed[g, pl.ds(head, tokens, stride=heads), :] for g in range(latent // lanes)],
            axis=1,
        ).astype(BF16)
        at = slice(head * vdim, (head + 1) * vdim)
        value = residual[:, at].astype(F32) + jnp.dot(
            part, up[head], preferred_element_type=F32
        )
        stream[:, at] = value
        square = square + jnp.sum(value * value, axis=-1, keepdims=True)
    factor = lax.rsqrt(square / features + 1e-06)
    normed[:, :features] = (stream[...] * factor * gain[...]).astype(BF16)
    normed[:, features:] = packed(routes[...], shares[...], tokens)


def packed(routes, shares, tokens):
    top = routes.shape[0]
    first = shares.astype(BF16).astype(F32)
    second = (shares - first).astype(BF16).astype(F32)
    third = shares - first - second
    rows = jnp.concatenate([routes.astype(F32), first, second, third], axis=1)
    rest = jnp.zeros((tokens - top, rows.shape[1]), F32)
    return jnp.concatenate([rows, rest], axis=0).astype(BF16)


def unpacked(block, top, tokens):
    rows = block[...].astype(F32)[:top]
    parts = [rows[:, i * tokens : (i + 1) * tokens] for i in range(4)]
    return parts[0], parts[1] + parts[2] + parts[3]


def attend(queries, cache, drafts, lengths, value_up, residual, norm_gain, routes, shares):
    reqs, draft, heads, width = queries.shape
    slots = cache.shape[1]
    latent, vdim = value_up.shape[1:]
    tokens, features = residual.shape
    rows = draft * heads
    flops = 2 * reqs * rows * slots * (width + latent) + 2 * tokens * heads * latent * vdim
    operands = (
        lengths,
        drafts,
        queries.reshape(reqs, rows, width),
        jnp.swapaxes(cache, 1, 2),
        value_up,
        residual,
        norm_gain.reshape(1, features),
        routes,
        shares,
    )
    held = [pltpu.VMEM(o.shape, o.dtype) for o in operands]
    held[0] = pltpu.SMEM(lengths.shape, jnp.int32)
    held[3] = pltpu.VMEM((reqs, width, (slots + draft + 127) // 128 * 128), BF16)
    return pl.pallas_call(
        functools.partial(attend_kernel, heads),
        in_specs=[pl.BlockSpec(memory_space=pltpu.HBM)] * 9,
        out_specs=[whole()] * 2,
        out_shape=[
            jax.ShapeDtypeStruct((tokens, features), F32),
            jax.ShapeDtypeStruct((tokens, features + 4 * tokens), BF16),
        ],
        scratch_shapes=held
        + [
            pltpu.VMEM((latent // 128, reqs * rows, 128), F32),
            pltpu.SemaphoreType.DMA((2 * reqs + 7,)),
        ],
        cost_estimate=pl.CostEstimate(
            flops=flops, bytes_accessed=6 * MIB, transcendentals=reqs * rows * slots
        ),
        compiler_params=pltpu.CompilerParams(vmem_limit_bytes=60 * MIB),
    )(*operands)


def dispatch_kernel(top, stride, mine, here, there, high, low, *refs):
    blocks, table = refs[:-1], refs[-1]
    tokens, features = here.shape[0], blocks[0].shape[1]
    here_routes, here_shares = unpacked(here.at[:, features:], top, tokens)
    there_routes, there_shares = unpacked(there.at[:, features:], top, tokens)
    routes = jnp.concatenate([here_routes, there_routes], axis=1)
    shares = jnp.concatenate([here_shares, there_shares], axis=1)
    experts = mine[...]
    both = 2 * tokens
    count = experts.shape[0]
    named = jnp.zeros((count, both), F32)
    weight = jnp.zeros((count, both), F32)
    for k in range(top):
        hit = jnp.where(routes[k : k + 1, :] == experts, 1.0, 0.0)
        named = named + hit
        weight = weight + hit * shares[k : k + 1, :]
    earlier = lax.broadcasted_iota(jnp.int32, (both, both), 0)
    later = lax.broadcasted_iota(jnp.int32, (both, both), 1)
    before = (earlier < later) & ((earlier < tokens) == (later < tokens))
    rank = jnp.dot(
        named.astype(BF16),
        jnp.where(before, 1.0, 0.0).astype(BF16),
        preferred_element_type=F32,
    )
    behind = lax.broadcasted_iota(jnp.int32, (count, both), 1) >= tokens
    place = rank.astype(jnp.int32) + jnp.where(behind, stride, 0)
    place = jnp.where(named > 0.0, place, -1)
    slots = lax.broadcasted_iota(jnp.int32, (2 * stride, both), 0)
    rows = jnp.concatenate([here[:, :features], there[:, :features]], axis=0)
    for m, block in enumerate(blocks):
        hit = jnp.where(slots == place[m : m + 1, :], 1.0, 0.0)
        table[2 * stride * m : 2 * stride * (m + 1), :] = hit * weight[m : m + 1, :]
        block[...] = jnp.dot(hit.astype(BF16), rows, preferred_element_type=F32).astype(BF16)
    turned = table[...].T
    top_bits = turned.astype(BF16)
    high[...] = top_bits
    low[...] = (turned - top_bits.astype(F32)).astype(BF16)


def dispatch(mine, here, there, top, stride):
    count, both = mine.shape[0], 2 * here.shape[0]
    width = here.shape[1] - 2 * both
    rows = count * 2 * stride
    return pl.pallas_call(
        functools.partial(dispatch_kernel, top, stride),
        in_specs=[whole()] * 3,
        out_specs=[whole()] * (2 + count),
        out_shape=[jax.ShapeDtypeStruct((both, rows), BF16)] * 2
        + [jax.ShapeDtypeStruct((2 * stride, width), BF16)] * count,
        scratch_shapes=[pltpu.VMEM((rows, both), F32)],
        cost_estimate=pl.CostEstimate(
            flops=2 * rows * both * width, bytes_accessed=3 * MIB // 2, transcendentals=0
        ),
        compiler_params=pltpu.CompilerParams(vmem_limit_bytes=16 * MIB),
    )(mine, here, there)


def load_kernel(*refs):
    count = len(refs) // 2
    sems = refs[-1]
    copies = [
        pltpu.make_async_copy(refs[i], refs[count + i], sems.at[i]) for i in range(count)
    ]
    for copy in copies:
        copy.start()
    for copy in copies:
        copy.wait()


def load(weights, room):
    return pl.pallas_call(
        load_kernel,
        in_specs=[pl.BlockSpec(memory_space=pl.ANY)] * len(weights),
        out_specs=[whole()] * len(weights),
        out_shape=[jax.ShapeDtypeStruct(w.shape, w.dtype) for w in weights],
        scratch_shapes=[pltpu.SemaphoreType.DMA((len(weights),))],
        cost_estimate=pl.CostEstimate(
            flops=0, bytes_accessed=2 * sum(2 * w.size for w in weights), transcendentals=0
        ),
        compiler_params=pltpu.CompilerParams(vmem_limit_bytes=room * MIB),
    )(*weights)


def expert_kernel(count, *refs):
    blocks = refs[:count]
    near, far = refs[count : count + 3], refs[count + 3 : count + 6]
    outs = refs[count + 6 : 2 * count + 6]
    held = refs[2 * count + 6 : 2 * count + 8]
    rows_ref, total, sems = refs[2 * count + 8 :]
    copies = {i: pltpu.make_async_copy(far[i], held[i - 1], sems.at[i - 1]) for i in (1, 2)}
    for i in (1, 2):
        copies[i].start()
    size = blocks[0].shape[0]
    for m, block in enumerate(blocks):
        rows_ref[m * size : (m + 1) * size, :] = block[...]

    def half(weights, ready):
        w_gate, w_up, w_down = weights
        ready(0)
        gate = lax.dot_general(rows_ref[...], w_gate[...], NT, preferred_element_type=F32)
        ready(1)
        upper = lax.dot_general(rows_ref[...], w_up[...], NT, preferred_element_type=F32)
        active = (gate * (1.0 / (1.0 + jnp.exp(-gate))) * upper).astype(BF16)
        ready(2)
        return jnp.dot(active, w_down[...], preferred_element_type=F32)

    total[...] = half(near, lambda i: None)
    far_half = half((far[0], *held), lambda i: i and copies[i].wait())
    result = (total[...] + far_half).astype(BF16)
    for m, out in enumerate(outs):
        out[...] = result[m * size : (m + 1) * size, :]


def run_expert(blocks, near, far):
    count = len(blocks)
    size, width = blocks[0].shape
    units = near[0].shape[0]
    return pl.pallas_call(
        functools.partial(expert_kernel, count),
        in_specs=[whole()] * (count + 4) + [pl.BlockSpec(memory_space=pl.ANY)] * 2,
        out_specs=[whole()] * count,
        out_shape=[jax.ShapeDtypeStruct((size, width), BF16)] * count,
        scratch_shapes=[pltpu.VMEM((units, width), BF16)] * 2
        + [
            pltpu.VMEM((count * size, width), BF16),
            pltpu.VMEM((count * size, width), F32),
            pltpu.SemaphoreType.DMA((2,)),
        ],
        cost_estimate=pl.CostEstimate(
            flops=12 * count * size * width * units,
            bytes_accessed=12 * units * width,
            transcendentals=2 * count * size * units,
        ),
        compiler_params=pltpu.CompilerParams(vmem_limit_bytes=36 * MIB),
    )(*blocks, *near, *far)


def combine_kernel(high, low, *refs):
    blocks, (here, there) = refs[:-2], refs[-2:]
    rows = jnp.concatenate([block[...] for block in blocks], axis=0)
    total = jnp.dot(high[...], rows, preferred_element_type=F32)
    total = total + jnp.dot(low[...], rows, preferred_element_type=F32)
    tokens = here.shape[0]
    here[...] = total[:tokens]
    there[...] = total[tokens:].astype(BF16)


def combine(high, low, blocks):
    both, rows = high.shape
    width = blocks[0].shape[1]
    return pl.pallas_call(
        combine_kernel,
        in_specs=[whole()] * (2 + len(blocks)),
        out_specs=[whole()] * 2,
        out_shape=[
            jax.ShapeDtypeStruct((both // 2, width), F32),
            jax.ShapeDtypeStruct((both // 2, width), BF16),
        ],
        cost_estimate=pl.CostEstimate(
            flops=4 * both * rows * width, bytes_accessed=3 * MIB // 2, transcendentals=0
        ),
        compiler_params=pltpu.CompilerParams(vmem_limit_bytes=16 * MIB),
    )(high, low, *blocks)


def local(
    queries,
    cache,
    drafts,
    lengths,
    value_up,
    residual,
    norm_gain,
    w_gate,
    w_up,
    w_down,
    routes,
    combine_weights,
):
    tokens, top = routes.shape
    devices = lax.axis_size("ep")
    experts = devices // 2
    near = experts // 2
    capacity = min(tokens, 2 * (((tokens * top + experts - 1) // experts + 3) // 2))
    stride = -(-capacity // 8) * 8

    own = [jnp.swapaxes(w_gate, 1, 2)[0], jnp.swapaxes(w_up, 1, 2)[0], w_down[0]]
    other = [swapped(w, 1) for w in own]
    chip = lax.axis_index("ep") // 2
    mine = (chip ^ jnp.arange(near - 1, -1, -1, dtype=jnp.int32)).astype(F32)[:, None]

    stream, normed = attend(
        queries, cache, drafts, lengths, value_up, residual, norm_gain, routes.T, combine_weights.T
    )
    normed, own = lax.optimization_barrier((normed, own))
    across = swapped(normed, devices // 2)
    own = load(own, 44)
    across, own, other = lax.optimization_barrier((across, own, other))
    high, low, *blocks = dispatch(mine, normed, across, top, stride)
    blocks = exchanged(blocks)
    blocks = exchanged(run_expert(blocks, own, other))
    here, there = combine(high, low, blocks)
    return (stream + (here + swapped(there, devices // 2).astype(F32))).astype(BF16)


def solution(mesh):
    placed = (
        P(("groups", "ep"), None, None, None),
        P(("groups", "ep"), None, None),
        P(("groups", "ep"), None, None),
        P(("groups", "ep")),
        P(),
        P(("groups", "ep"), None),
        P(),
        P("ep", None, None),
        P("ep", None, None),
        P("ep", None, None),
        P(("groups", "ep"), None),
        P(("groups", "ep"), None),
    )
    return jax.shard_map(
        local, mesh=mesh, in_specs=placed, out_specs=P(("groups", "ep"), None), check_vma=False
    )
```

```python
import functools

import jax
import jax.numpy as jnp
from jax import lax
from jax.experimental import pallas as pl
from jax.experimental.pallas import tpu as pltpu
from jax.sharding import PartitionSpec as P

F32 = jnp.float32
BF16 = jnp.bfloat16
NT = (((1,), (1,)), ((), ()))
MIB = 1 << 20


def swapped(value, mask):
    pairs = [(source, source ^ mask) for source in range(lax.axis_size("ep"))]
    return lax.ppermute(value, "ep", pairs)


def exchanged(blocks):
    last = len(blocks) - 1
    return [swapped(b, 2 * (last - i)) if i < last else b for i, b in enumerate(blocks)]


def whole():
    return pl.BlockSpec(memory_space=pltpu.VMEM)


def attend_kernel(heads, *refs):
    given, (stream, normed), held = refs[:9], refs[9:11], refs[11:20]
    mixed, sems = refs[20:]
    lengths, drafts, queries, cache, up, residual, gain, routes, shares = held
    reqs, rows, width = queries.shape
    slots = given[3].shape[2]
    draft = drafts.shape[1]
    latent, vdim = up.shape[1:]
    lanes = mixed.shape[2]
    columns = cache.shape[2]
    copies = {}
    order = [(0, None), (1, None)] + [(i, r) for r in range(reqs) for i in (2, 3)]
    for n, (i, r) in enumerate(order + [(i, None) for i in range(4, 9)]):
        source, target = (given[i], held[i]) if r is None else (given[i].at[r], held[i].at[r])
        if i == 3:
            target = target.at[:, :slots]
        copies[i, r] = pltpu.make_async_copy(source, target, sems.at[n])
        copies[i, r].start()
    scale = (vdim + width - latent) ** (-0.5)
    place = lax.broadcasted_iota(jnp.int32, (rows, columns), 1)
    token = lax.broadcasted_iota(jnp.int32, (rows, columns), 0) // heads
    causal = (place >= slots) & (place - slots <= token)
    copies[0, None].wait()
    copies[1, None].wait()
    for r in range(reqs):
        d = jnp.concatenate(
            [drafts[r].astype(F32), jnp.zeros((columns - slots - draft, width), F32)], axis=0
        )
        cache[r, :, slots:] = d.T.astype(BF16)
    for r in range(reqs):
        copies[2, r].wait()
        copies[3, r].wait()
        score = jnp.dot(queries[r], cache[r], preferred_element_type=F32) * scale
        score = jnp.where((place < lengths[r]) | causal, score, -1e30)
        e = jnp.exp(score - jnp.max(score, axis=-1, keepdims=True))
        p = (e * (1.0 / jnp.sum(e, axis=-1, keepdims=True))).astype(BF16)
        out = lax.dot_general(p, cache[r, :latent, :], NT, preferred_element_type=F32)
        for g in range(latent // lanes):
            mixed[g, r * rows : (r + 1) * rows, :] = out[:, g * lanes : (g + 1) * lanes]
    for i in range(4, 9):
        copies[i, None].wait()
    tokens, features = stream.shape
    square = jnp.zeros((tokens, 1), F32)
    for head in range(heads):
        part = jnp.concatenate(
            [mixed[g, pl.ds(head, tokens, stride=heads), :] for g in range(latent // lanes)],
            axis=1,
        ).astype(BF16)
        at = slice(head * vdim, (head + 1) * vdim)
        value = residual[:, at].astype(F32) + jnp.dot(
            part, up[head], preferred_element_type=F32
        )
        stream[:, at] = value
        square = square + jnp.sum(value * value, axis=-1, keepdims=True)
    factor = lax.rsqrt(square / features + 1e-06)
    normed[:, :features] = (stream[...] * factor * gain[...]).astype(BF16)
    normed[:, features:] = packed(routes[...], shares[...], tokens)


def packed(routes, shares, tokens):
    top = routes.shape[0]
    first = shares.astype(BF16).astype(F32)
    second = (shares - first).astype(BF16).astype(F32)
    third = shares - first - second
    rows = jnp.concatenate([routes.astype(F32), first, second, third], axis=1)
    rest = jnp.zeros((tokens - top, rows.shape[1]), F32)
    return jnp.concatenate([rows, rest], axis=0).astype(BF16)


def unpacked(block, top, tokens):
    rows = block[...].astype(F32)[:top]
    parts = [rows[:, i * tokens : (i + 1) * tokens] for i in range(4)]
    return parts[0], parts[1] + parts[2] + parts[3]


def attend(queries, cache, drafts, lengths, value_up, residual, norm_gain, routes, shares):
    reqs, draft, heads, width = queries.shape
    slots = cache.shape[1]
    latent, vdim = value_up.shape[1:]
    tokens, features = residual.shape
    rows = draft * heads
    flops = 2 * reqs * rows * slots * (width + latent) + 2 * tokens * heads * latent * vdim
    operands = (
        lengths,
        drafts,
        queries.reshape(reqs, rows, width),
        jnp.swapaxes(cache, 1, 2),
        value_up,
        residual,
        norm_gain.reshape(1, features),
        routes,
        shares,
    )
    held = [pltpu.VMEM(o.shape, o.dtype) for o in operands]
    held[0] = pltpu.SMEM(lengths.shape, jnp.int32)
    held[3] = pltpu.VMEM((reqs, width, (slots + draft + 127) // 128 * 128), BF16)
    return pl.pallas_call(
        functools.partial(attend_kernel, heads),
        in_specs=[pl.BlockSpec(memory_space=pltpu.HBM)] * 9,
        out_specs=[whole()] * 2,
        out_shape=[
            jax.ShapeDtypeStruct((tokens, features), F32),
            jax.ShapeDtypeStruct((tokens, features + 4 * tokens), BF16),
        ],
        scratch_shapes=held
        + [
            pltpu.VMEM((latent // 128, reqs * rows, 128), F32),
            pltpu.SemaphoreType.DMA((2 * reqs + 7,)),
        ],
        cost_estimate=pl.CostEstimate(
            flops=flops, bytes_accessed=6 * MIB, transcendentals=reqs * rows * slots
        ),
        compiler_params=pltpu.CompilerParams(vmem_limit_bytes=56 * MIB),
    )(*operands)


def dispatch_kernel(top, stride, mine, here, there, high, low, *refs):
    blocks, table = refs[:-1], refs[-1]
    tokens, features = here.shape[0], blocks[0].shape[1]
    here_routes, here_shares = unpacked(here.at[:, features:], top, tokens)
    there_routes, there_shares = unpacked(there.at[:, features:], top, tokens)
    routes = jnp.concatenate([here_routes, there_routes], axis=1)
    shares = jnp.concatenate([here_shares, there_shares], axis=1)
    experts = mine[...]
    both = 2 * tokens
    count = experts.shape[0]
    named = jnp.zeros((count, both), F32)
    weight = jnp.zeros((count, both), F32)
    for k in range(top):
        hit = jnp.where(routes[k : k + 1, :] == experts, 1.0, 0.0)
        named = named + hit
        weight = weight + hit * shares[k : k + 1, :]
    earlier = lax.broadcasted_iota(jnp.int32, (both, both), 0)
    later = lax.broadcasted_iota(jnp.int32, (both, both), 1)
    before = (earlier < later) & ((earlier < tokens) == (later < tokens))
    rank = jnp.dot(
        named.astype(BF16),
        jnp.where(before, 1.0, 0.0).astype(BF16),
        preferred_element_type=F32,
    )
    behind = lax.broadcasted_iota(jnp.int32, (count, both), 1) >= tokens
    place = rank.astype(jnp.int32) + jnp.where(behind, stride, 0)
    place = jnp.where(named > 0.0, place, -1)
    slots = lax.broadcasted_iota(jnp.int32, (2 * stride, both), 0)
    rows = jnp.concatenate([here[:, :features], there[:, :features]], axis=0)
    for m, block in enumerate(blocks):
        hit = jnp.where(slots == place[m : m + 1, :], 1.0, 0.0)
        table[2 * stride * m : 2 * stride * (m + 1), :] = hit * weight[m : m + 1, :]
        block[...] = jnp.dot(hit.astype(BF16), rows, preferred_element_type=F32).astype(BF16)
    turned = table[...].T
    top_bits = turned.astype(BF16)
    high[...] = top_bits
    low[...] = (turned - top_bits.astype(F32)).astype(BF16)


def dispatch(mine, here, there, top, stride):
    count, both = mine.shape[0], 2 * here.shape[0]
    width = here.shape[1] - 2 * both
    rows = count * 2 * stride
    return pl.pallas_call(
        functools.partial(dispatch_kernel, top, stride),
        in_specs=[whole()] * 3,
        out_specs=[whole()] * (2 + count),
        out_shape=[jax.ShapeDtypeStruct((both, rows), BF16)] * 2
        + [jax.ShapeDtypeStruct((2 * stride, width), BF16)] * count,
        scratch_shapes=[pltpu.VMEM((rows, both), F32)],
        cost_estimate=pl.CostEstimate(
            flops=2 * rows * both * width, bytes_accessed=3 * MIB // 2, transcendentals=0
        ),
        compiler_params=pltpu.CompilerParams(vmem_limit_bytes=16 * MIB),
    )(mine, here, there)


def load_kernel(*refs):
    count = len(refs) // 2
    sems = refs[-1]
    copies = [
        pltpu.make_async_copy(refs[i], refs[count + i], sems.at[i]) for i in range(count)
    ]
    for copy in copies:
        copy.start()
    for copy in copies:
        copy.wait()


def load(weights, room):
    return pl.pallas_call(
        load_kernel,
        in_specs=[pl.BlockSpec(memory_space=pl.ANY)] * len(weights),
        out_specs=[whole()] * len(weights),
        out_shape=[jax.ShapeDtypeStruct(w.shape, w.dtype) for w in weights],
        scratch_shapes=[pltpu.SemaphoreType.DMA((len(weights),))],
        cost_estimate=pl.CostEstimate(
            flops=0, bytes_accessed=2 * sum(2 * w.size for w in weights), transcendentals=0
        ),
        compiler_params=pltpu.CompilerParams(vmem_limit_bytes=room * MIB),
    )(*weights)


def expert_kernel(count, *refs):
    blocks, weights = refs[:count], refs[count : count + 6]
    outs = refs[count + 6 : 2 * count + 6]
    rows, active = refs[2 * count + 6 :]
    size, width = blocks[0].shape
    for m, block in enumerate(blocks):
        rows[m * size : (m + 1) * size, :] = block[...]
    for half in range(2):
        w_gate, w_up = weights[3 * half : 3 * half + 2]
        gate = lax.dot_general(rows[...], w_gate[...], NT, preferred_element_type=F32)
        upper = lax.dot_general(rows[...], w_up[...], NT, preferred_element_type=F32)
        active[half] = (gate * (1.0 / (1.0 + jnp.exp(-gate))) * upper).astype(BF16)
    for at in range(0, width, 512):
        columns = slice(at, at + 512)
        result = jnp.dot(active[0], weights[2][:, columns], preferred_element_type=F32)
        result = result + jnp.dot(active[1], weights[5][:, columns], preferred_element_type=F32)
        for m, out in enumerate(outs):
            out[:, columns] = result[m * size : (m + 1) * size, :].astype(BF16)


def run_expert(blocks, weights):
    count = len(blocks)
    size, width = blocks[0].shape
    units = weights[0].shape[0]
    return pl.pallas_call(
        functools.partial(expert_kernel, count),
        in_specs=[whole()] * (count + 6),
        out_specs=[whole()] * count,
        out_shape=[jax.ShapeDtypeStruct((size, width), BF16)] * count,
        scratch_shapes=[
            pltpu.VMEM((count * size, width), BF16),
            pltpu.VMEM((2, count * size, units), BF16),
        ],
        cost_estimate=pl.CostEstimate(
            flops=12 * count * size * width * units,
            bytes_accessed=12 * units * width,
            transcendentals=2 * count * size * units,
        ),
        compiler_params=pltpu.CompilerParams(vmem_limit_bytes=20 * MIB),
    )(*blocks, *weights)


def combine_kernel(high, low, *refs):
    blocks, (here, there) = refs[:-2], refs[-2:]
    rows = jnp.concatenate([block[...] for block in blocks], axis=0)
    total = jnp.dot(high[...], rows, preferred_element_type=F32)
    total = total + jnp.dot(low[...], rows, preferred_element_type=F32)
    tokens = here.shape[0]
    here[...] = total[:tokens]
    there[...] = total[tokens:].astype(BF16)


def combine(high, low, blocks):
    both, rows = high.shape
    width = blocks[0].shape[1]
    return pl.pallas_call(
        combine_kernel,
        in_specs=[whole()] * (2 + len(blocks)),
        out_specs=[whole()] * 2,
        out_shape=[
            jax.ShapeDtypeStruct((both // 2, width), F32),
            jax.ShapeDtypeStruct((both // 2, width), BF16),
        ],
        cost_estimate=pl.CostEstimate(
            flops=4 * both * rows * width, bytes_accessed=3 * MIB // 2, transcendentals=0
        ),
        compiler_params=pltpu.CompilerParams(vmem_limit_bytes=16 * MIB),
    )(high, low, *blocks)


def local(
    queries,
    cache,
    drafts,
    lengths,
    value_up,
    residual,
    norm_gain,
    w_gate,
    w_up,
    w_down,
    routes,
    combine_weights,
):
    tokens, top = routes.shape
    devices = lax.axis_size("ep")
    experts = devices // 2
    near = experts // 2
    capacity = min(tokens, 2 * (((tokens * top + experts - 1) // experts + 3) // 2))
    stride = -(-capacity // 8) * 8

    own = [jnp.swapaxes(w_gate, 1, 2)[0], jnp.swapaxes(w_up, 1, 2)[0], w_down[0]]
    other = [swapped(w, 1) for w in own]
    chip = lax.axis_index("ep") // 2
    mine = (chip ^ jnp.arange(near - 1, -1, -1, dtype=jnp.int32)).astype(F32)[:, None]

    stream, normed = attend(
        queries, cache, drafts, lengths, value_up, residual, norm_gain, routes.T, combine_weights.T
    )
    normed, own = lax.optimization_barrier((normed, own))
    across = swapped(normed, devices // 2)
    own = load(own, 44)
    across, own, other = lax.optimization_barrier((across, own, other))
    high, low, *blocks = dispatch(mine, normed, across, top, stride)
    blocks = exchanged(blocks)
    blocks[2], *late = lax.optimization_barrier((blocks[2], *other[1:]))
    blocks = exchanged(run_expert(blocks, [*own, other[0], *load(late, 38)]))
    here, there = combine(high, low, blocks)
    return (stream + (here + swapped(there, devices // 2).astype(F32))).astype(BF16)


def solution(mesh):
    placed = (
        P(("groups", "ep"), None, None, None),
        P(("groups", "ep"), None, None),
        P(("groups", "ep"), None, None),
        P(("groups", "ep")),
        P(),
        P(("groups", "ep"), None),
        P(),
        P("ep", None, None),
        P("ep", None, None),
        P("ep", None, None),
        P(("groups", "ep"), None),
        P(("groups", "ep"), None),
    )
    return jax.shard_map(
        local, mesh=mesh, in_specs=placed, out_specs=P(("groups", "ep"), None), check_vma=False
    )
```

```python
import functools

import jax
import jax.numpy as jnp
from jax import lax
from jax.experimental import pallas as pl
from jax.experimental.pallas import tpu as pltpu
from jax.sharding import PartitionSpec as P

F32 = jnp.float32
BF16 = jnp.bfloat16
NT = (((1,), (1,)), ((), ()))
MIB = 1 << 20


def swapped(value, mask):
    pairs = [(source, source ^ mask) for source in range(lax.axis_size("ep"))]
    return lax.ppermute(value, "ep", pairs)


def exchanged(blocks):
    last = len(blocks) - 1
    return [swapped(b, 2 * (last - i)) if i < last else b for i, b in enumerate(blocks)]


def returned(rows, near):
    groups = [
        [first + 2 * i + core for i in range(near)]
        for first in range(0, lax.axis_size("ep"), 2 * near)
        for core in range(2)
    ]
    blocks = rows.reshape(near, rows.shape[0] // near, rows.shape[1])
    got = lax.all_to_all(
        blocks, "ep", split_axis=0, concat_axis=0, tiled=True, axis_index_groups=groups
    )
    return got.reshape(rows.shape)


def block_of(place, count, size):
    local = (lax.axis_index("ep") // 2) % count
    return pl.ds(pl.multiple_of((local ^ (count - 1 - place)) * size, size), size)


def whole():
    return pl.BlockSpec(memory_space=pltpu.VMEM)


def attend_kernel(heads, *refs):
    given, (stream, normed), held = refs[:9], refs[9:11], refs[11:20]
    mixed, sems = refs[20:]
    lengths, drafts, queries, cache, up, residual, gain, routes, shares = held
    reqs, rows, width = queries.shape
    slots = given[3].shape[2]
    draft = drafts.shape[1]
    latent, vdim = up.shape[1:]
    lanes = mixed.shape[2]
    columns = cache.shape[2]
    copies = {}
    order = [(0, None), (1, None)] + [(i, r) for r in range(reqs) for i in (2, 3)]
    for n, (i, r) in enumerate(order + [(i, None) for i in range(4, 9)]):
        source, target = (given[i], held[i]) if r is None else (given[i].at[r], held[i].at[r])
        if i == 3:
            target = target.at[:, :slots]
        copies[i, r] = pltpu.make_async_copy(source, target, sems.at[n])
        copies[i, r].start()
    scale = (vdim + width - latent) ** (-0.5)
    place = lax.broadcasted_iota(jnp.int32, (rows, columns), 1)
    token = lax.broadcasted_iota(jnp.int32, (rows, columns), 0) // heads
    causal = (place >= slots) & (place - slots <= token)
    copies[0, None].wait()
    copies[1, None].wait()
    for r in range(reqs):
        d = jnp.concatenate(
            [drafts[r].astype(F32), jnp.zeros((columns - slots - draft, width), F32)], axis=0
        )
        cache[r, :, slots:] = d.T.astype(BF16)
    for r in range(reqs):
        copies[2, r].wait()
        copies[3, r].wait()
        score = jnp.dot(queries[r], cache[r], preferred_element_type=F32) * scale
        score = jnp.where((place < lengths[r]) | causal, score, -1e30)
        e = jnp.exp(score - jnp.max(score, axis=-1, keepdims=True))
        p = (e * (1.0 / jnp.sum(e, axis=-1, keepdims=True))).astype(BF16)
        out = lax.dot_general(p, cache[r, :latent, :], NT, preferred_element_type=F32)
        for g in range(latent // lanes):
            mixed[g, r * rows : (r + 1) * rows, :] = out[:, g * lanes : (g + 1) * lanes]
    for i in range(4, 9):
        copies[i, None].wait()
    tokens, features = stream.shape
    square = jnp.zeros((tokens, 1), F32)
    for head in range(heads):
        part = jnp.concatenate(
            [mixed[g, pl.ds(head, tokens, stride=heads), :] for g in range(latent // lanes)],
            axis=1,
        ).astype(BF16)
        at = slice(head * vdim, (head + 1) * vdim)
        value = residual[:, at].astype(F32) + jnp.dot(
            part, up[head], preferred_element_type=F32
        )
        stream[:, at] = value
        square = square + jnp.sum(value * value, axis=-1, keepdims=True)
    factor = lax.rsqrt(square / features + 1e-06)
    normed[:, :features] = (stream[...] * factor * gain[...]).astype(BF16)
    normed[:, features:] = packed(routes[...], shares[...], tokens)


def packed(routes, shares, tokens):
    top = routes.shape[0]
    first = shares.astype(BF16).astype(F32)
    second = (shares - first).astype(BF16).astype(F32)
    third = shares - first - second
    rows = jnp.concatenate([routes.astype(F32), first, second, third], axis=1)
    rest = jnp.zeros((tokens - top, rows.shape[1]), F32)
    return jnp.concatenate([rows, rest], axis=0).astype(BF16)


def unpacked(block, top, tokens):
    rows = block[...].astype(F32)[:top]
    parts = [rows[:, i * tokens : (i + 1) * tokens] for i in range(4)]
    return parts[0], parts[1] + parts[2] + parts[3]


def attend(queries, cache, drafts, lengths, value_up, residual, norm_gain, routes, shares):
    reqs, draft, heads, width = queries.shape
    slots = cache.shape[1]
    latent, vdim = value_up.shape[1:]
    tokens, features = residual.shape
    rows = draft * heads
    flops = 2 * reqs * rows * slots * (width + latent) + 2 * tokens * heads * latent * vdim
    operands = (
        lengths,
        drafts,
        queries.reshape(reqs, rows, width),
        jnp.swapaxes(cache, 1, 2),
        value_up,
        residual,
        norm_gain.reshape(1, features),
        routes,
        shares,
    )
    held = [pltpu.VMEM(o.shape, o.dtype) for o in operands]
    held[0] = pltpu.SMEM(lengths.shape, jnp.int32)
    held[3] = pltpu.VMEM((reqs, width, (slots + draft + 127) // 128 * 128), BF16)
    return pl.pallas_call(
        functools.partial(attend_kernel, heads),
        in_specs=[pl.BlockSpec(memory_space=pltpu.HBM)] * 9,
        out_specs=[whole()] * 2,
        out_shape=[
            jax.ShapeDtypeStruct((tokens, features), F32),
            jax.ShapeDtypeStruct((tokens, features + 4 * tokens), BF16),
        ],
        scratch_shapes=held
        + [
            pltpu.VMEM((latent // 128, reqs * rows, 128), F32),
            pltpu.SemaphoreType.DMA((2 * reqs + 7,)),
        ],
        cost_estimate=pl.CostEstimate(
            flops=flops, bytes_accessed=6 * MIB, transcendentals=reqs * rows * slots
        ),
        compiler_params=pltpu.CompilerParams(vmem_limit_bytes=56 * MIB),
    )(*operands)


def dispatch_kernel(top, stride, mine, here, there, high, low, *refs):
    blocks, table = refs[:-1], refs[-1]
    tokens, features = here.shape[0], blocks[0].shape[1]
    here_routes, here_shares = unpacked(here.at[:, features:], top, tokens)
    there_routes, there_shares = unpacked(there.at[:, features:], top, tokens)
    routes = jnp.concatenate([here_routes, there_routes], axis=1)
    shares = jnp.concatenate([here_shares, there_shares], axis=1)
    experts = mine[...]
    both = 2 * tokens
    count = experts.shape[0]
    named = jnp.zeros((count, both), F32)
    weight = jnp.zeros((count, both), F32)
    for k in range(top):
        hit = jnp.where(routes[k : k + 1, :] == experts, 1.0, 0.0)
        named = named + hit
        weight = weight + hit * shares[k : k + 1, :]
    earlier = lax.broadcasted_iota(jnp.int32, (both, both), 0)
    later = lax.broadcasted_iota(jnp.int32, (both, both), 1)
    before = (earlier < later) & ((earlier < tokens) == (later < tokens))
    rank = jnp.dot(
        named.astype(BF16),
        jnp.where(before, 1.0, 0.0).astype(BF16),
        preferred_element_type=F32,
    )
    behind = lax.broadcasted_iota(jnp.int32, (count, both), 1) >= tokens
    place = rank.astype(jnp.int32) + jnp.where(behind, stride, 0)
    place = jnp.where(named > 0.0, place, -1)
    slots = lax.broadcasted_iota(jnp.int32, (2 * stride, both), 0)
    rows = jnp.concatenate([here[:, :features], there[:, :features]], axis=0)
    for m, block in enumerate(blocks):
        hit = jnp.where(slots == place[m : m + 1, :], 1.0, 0.0)
        table[block_of(m, count, 2 * stride), :] = hit * weight[m : m + 1, :]
        block[...] = jnp.dot(hit.astype(BF16), rows, preferred_element_type=F32).astype(BF16)
    turned = table[...].T
    top_bits = turned.astype(BF16)
    high[...] = top_bits
    low[...] = (turned - top_bits.astype(F32)).astype(BF16)


def dispatch(mine, here, there, top, stride):
    count, both = mine.shape[0], 2 * here.shape[0]
    width = here.shape[1] - 2 * both
    rows = count * 2 * stride
    return pl.pallas_call(
        functools.partial(dispatch_kernel, top, stride),
        in_specs=[whole()] * 3,
        out_specs=[whole()] * (2 + count),
        out_shape=[jax.ShapeDtypeStruct((both, rows), BF16)] * 2
        + [jax.ShapeDtypeStruct((2 * stride, width), BF16)] * count,
        scratch_shapes=[pltpu.VMEM((rows, both), F32)],
        cost_estimate=pl.CostEstimate(
            flops=2 * rows * both * width, bytes_accessed=3 * MIB // 2, transcendentals=0
        ),
        compiler_params=pltpu.CompilerParams(vmem_limit_bytes=16 * MIB),
    )(mine, here, there)


def load_kernel(*refs):
    count = len(refs) // 2
    sems = refs[-1]
    copies = [
        pltpu.make_async_copy(refs[i], refs[count + i], sems.at[i]) for i in range(count)
    ]
    for copy in copies:
        copy.start()
    for copy in copies:
        copy.wait()


def load(weights, room):
    return pl.pallas_call(
        load_kernel,
        in_specs=[pl.BlockSpec(memory_space=pl.ANY)] * len(weights),
        out_specs=[whole()] * len(weights),
        out_shape=[jax.ShapeDtypeStruct(w.shape, w.dtype) for w in weights],
        scratch_shapes=[pltpu.SemaphoreType.DMA((len(weights),))],
        cost_estimate=pl.CostEstimate(
            flops=0, bytes_accessed=2 * sum(2 * w.size for w in weights), transcendentals=0
        ),
        compiler_params=pltpu.CompilerParams(vmem_limit_bytes=room * MIB),
    )(*weights)


def expert_kernel(count, *refs):
    blocks, weights = refs[:count], refs[count : count + 6]
    out, rows, active = refs[count + 6 :]
    size, width = blocks[0].shape
    for m, block in enumerate(blocks):
        rows[m * size : (m + 1) * size, :] = block[...]
    for half in range(2):
        w_gate, w_up = weights[3 * half : 3 * half + 2]
        gate = lax.dot_general(rows[...], w_gate[...], NT, preferred_element_type=F32)
        upper = lax.dot_general(rows[...], w_up[...], NT, preferred_element_type=F32)
        active[half] = (gate * (1.0 / (1.0 + jnp.exp(-gate))) * upper).astype(BF16)
    for at in range(0, width, 512):
        columns = slice(at, at + 512)
        result = jnp.dot(active[0], weights[2][:, columns], preferred_element_type=F32)
        result = result + jnp.dot(active[1], weights[5][:, columns], preferred_element_type=F32)
        for m in range(count):
            part = result[m * size : (m + 1) * size, :]
            out[block_of(m, count, size), columns] = part.astype(BF16)


def run_expert(blocks, weights):
    count = len(blocks)
    size, width = blocks[0].shape
    units = weights[0].shape[0]
    return pl.pallas_call(
        functools.partial(expert_kernel, count),
        in_specs=[whole()] * (count + 6),
        out_specs=whole(),
        out_shape=jax.ShapeDtypeStruct((count * size, width), BF16),
        scratch_shapes=[
            pltpu.VMEM((count * size, width), BF16),
            pltpu.VMEM((2, count * size, units), BF16),
        ],
        cost_estimate=pl.CostEstimate(
            flops=12 * count * size * width * units,
            bytes_accessed=12 * units * width,
            transcendentals=2 * count * size * units,
        ),
        compiler_params=pltpu.CompilerParams(vmem_limit_bytes=20 * MIB),
    )(*blocks, *weights)


def combine_kernel(high, low, rows, here, there):
    total = jnp.dot(high[...], rows[...], preferred_element_type=F32)
    total = total + jnp.dot(low[...], rows[...], preferred_element_type=F32)
    tokens = here.shape[0]
    here[...] = total[:tokens]
    there[...] = total[tokens:].astype(BF16)


def combine(high, low, rows):
    both, width = high.shape[0], rows.shape[1]
    return pl.pallas_call(
        combine_kernel,
        in_specs=[whole()] * 3,
        out_specs=[whole()] * 2,
        out_shape=[
            jax.ShapeDtypeStruct((both // 2, width), F32),
            jax.ShapeDtypeStruct((both // 2, width), BF16),
        ],
        cost_estimate=pl.CostEstimate(
            flops=4 * high.size * width, bytes_accessed=3 * MIB // 2, transcendentals=0
        ),
        compiler_params=pltpu.CompilerParams(vmem_limit_bytes=16 * MIB),
    )(high, low, rows)


def local(
    queries,
    cache,
    drafts,
    lengths,
    value_up,
    residual,
    norm_gain,
    w_gate,
    w_up,
    w_down,
    routes,
    combine_weights,
):
    tokens, top = routes.shape
    devices = lax.axis_size("ep")
    experts = devices // 2
    near = experts // 2
    capacity = min(tokens, 2 * (((tokens * top + experts - 1) // experts + 3) // 2))
    stride = -(-capacity // 8) * 8

    own = [jnp.swapaxes(w_gate, 1, 2)[0], jnp.swapaxes(w_up, 1, 2)[0], w_down[0]]
    other = [swapped(w, 1) for w in own]
    chip = lax.axis_index("ep") // 2
    mine = (chip ^ jnp.arange(near - 1, -1, -1, dtype=jnp.int32)).astype(F32)[:, None]

    stream, normed = attend(
        queries, cache, drafts, lengths, value_up, residual, norm_gain, routes.T, combine_weights.T
    )
    normed, own = lax.optimization_barrier((normed, own))
    across = swapped(normed, devices // 2)
    own = load(own, 44)
    across, own, other = lax.optimization_barrier((across, own, other))
    high, low, *blocks = dispatch(mine, normed, across, top, stride)
    blocks = exchanged(blocks)
    blocks[2], *late = lax.optimization_barrier((blocks[2], *other[1:]))
    rows = returned(run_expert(blocks, [*own, other[0], *load(late, 38)]), near)
    here, there = combine(high, low, rows)
    return (stream + (here + swapped(there, devices // 2).astype(F32))).astype(BF16)


def solution(mesh):
    placed = (
        P(("groups", "ep"), None, None, None),
        P(("groups", "ep"), None, None),
        P(("groups", "ep"), None, None),
        P(("groups", "ep")),
        P(),
        P(("groups", "ep"), None),
        P(),
        P("ep", None, None),
        P("ep", None, None),
        P("ep", None, None),
        P(("groups", "ep"), None),
        P(("groups", "ep"), None),
    )
    return jax.shard_map(
        local, mesh=mesh, in_specs=placed, out_specs=P(("groups", "ep"), None), check_vma=False
    )
```

```python
import functools

import jax
import jax.numpy as jnp
from jax import lax
from jax.experimental import pallas as pl
from jax.experimental.pallas import tpu as pltpu
from jax.sharding import PartitionSpec as P

F32 = jnp.float32
BF16 = jnp.bfloat16
NT = (((1,), (1,)), ((), ()))
MIB = 1 << 20


def swapped(value, mask):
    pairs = [(source, source ^ mask) for source in range(lax.axis_size("ep"))]
    return lax.ppermute(value, "ep", pairs)


def orders(near):
    first = list(range(near - 1, -1, -1))
    return first, first[:1] + [(near - 1) ^ m for m in first[1:-1]] + [0]


def exchanged(blocks):
    got = list(blocks)
    for i, masks in enumerate(zip(*orders(len(blocks)))):
        pairs = [(d, d ^ 2 * masks[d % 2]) for d in range(lax.axis_size("ep"))]
        if any(masks):
            got[i] = lax.ppermute(blocks[i], "ep", pairs)
    return got


def whole():
    return pl.BlockSpec(memory_space=pltpu.VMEM)


def attend_kernel(heads, *refs):
    given, (stream, normed), held = refs[:9], refs[9:11], refs[11:20]
    mixed, sems = refs[20:]
    lengths, drafts, queries, cache, up, residual, gain, routes, shares = held
    reqs, rows, width = queries.shape
    slots = given[3].shape[2]
    draft = drafts.shape[1]
    latent, vdim = up.shape[1:]
    lanes = mixed.shape[2]
    columns = cache.shape[2]
    copies = {}
    order = [(0, None), (1, None)] + [(i, r) for r in range(reqs) for i in (2, 3)]
    for n, (i, r) in enumerate(order + [(i, None) for i in range(4, 9)]):
        source, target = (given[i], held[i]) if r is None else (given[i].at[r], held[i].at[r])
        if i == 3:
            target = target.at[:, :slots]
        copies[i, r] = pltpu.make_async_copy(source, target, sems.at[n])
        copies[i, r].start()
    scale = (vdim + width - latent) ** (-0.5)
    place = lax.broadcasted_iota(jnp.int32, (rows, columns), 1)
    token = lax.broadcasted_iota(jnp.int32, (rows, columns), 0) // heads
    causal = (place >= slots) & (place - slots <= token)
    copies[0, None].wait()
    copies[1, None].wait()
    for r in range(reqs):
        d = jnp.concatenate(
            [drafts[r].astype(F32), jnp.zeros((columns - slots - draft, width), F32)], axis=0
        )
        cache[r, :, slots:] = d.T.astype(BF16)
    for r in range(reqs):
        copies[2, r].wait()
        copies[3, r].wait()
        score = jnp.dot(queries[r], cache[r], preferred_element_type=F32) * scale
        score = jnp.where((place < lengths[r]) | causal, score, -1e30)
        e = jnp.exp(score - jnp.max(score, axis=-1, keepdims=True))
        p = (e * (1.0 / jnp.sum(e, axis=-1, keepdims=True))).astype(BF16)
        out = lax.dot_general(p, cache[r, :latent, :], NT, preferred_element_type=F32)
        for g in range(latent // lanes):
            mixed[g, r * rows : (r + 1) * rows, :] = out[:, g * lanes : (g + 1) * lanes]
    for i in range(4, 9):
        copies[i, None].wait()
    tokens, features = stream.shape
    square = jnp.zeros((tokens, 1), F32)
    for head in range(heads):
        part = jnp.concatenate(
            [mixed[g, pl.ds(head, tokens, stride=heads), :] for g in range(latent // lanes)],
            axis=1,
        ).astype(BF16)
        at = slice(head * vdim, (head + 1) * vdim)
        value = residual[:, at].astype(F32) + jnp.dot(
            part, up[head], preferred_element_type=F32
        )
        stream[:, at] = value
        square = square + jnp.sum(value * value, axis=-1, keepdims=True)
    factor = lax.rsqrt(square / features + 1e-06)
    normed[:, :features] = (stream[...] * factor * gain[...]).astype(BF16)
    normed[:, features:] = packed(routes[...], shares[...], tokens)


def packed(routes, shares, tokens):
    top = routes.shape[0]
    first = shares.astype(BF16).astype(F32)
    second = (shares - first).astype(BF16).astype(F32)
    third = shares - first - second
    rows = jnp.concatenate([routes.astype(F32), first, second, third], axis=1)
    rest = jnp.zeros((tokens - top, rows.shape[1]), F32)
    return jnp.concatenate([rows, rest], axis=0).astype(BF16)


def unpacked(block, top, tokens):
    rows = block[...].astype(F32)[:top]
    parts = [rows[:, i * tokens : (i + 1) * tokens] for i in range(4)]
    return parts[0], parts[1] + parts[2] + parts[3]


def attend(queries, cache, drafts, lengths, value_up, residual, norm_gain, routes, shares):
    reqs, draft, heads, width = queries.shape
    slots = cache.shape[1]
    latent, vdim = value_up.shape[1:]
    tokens, features = residual.shape
    rows = draft * heads
    flops = 2 * reqs * rows * slots * (width + latent) + 2 * tokens * heads * latent * vdim
    operands = (
        lengths,
        drafts,
        queries.reshape(reqs, rows, width),
        jnp.swapaxes(cache, 1, 2),
        value_up,
        residual,
        norm_gain.reshape(1, features),
        routes,
        shares,
    )
    held = [pltpu.VMEM(o.shape, o.dtype) for o in operands]
    held[0] = pltpu.SMEM(lengths.shape, jnp.int32)
    held[3] = pltpu.VMEM((reqs, width, (slots + draft + 127) // 128 * 128), BF16)
    return pl.pallas_call(
        functools.partial(attend_kernel, heads),
        in_specs=[pl.BlockSpec(memory_space=pltpu.HBM)] * 9,
        out_specs=[whole()] * 2,
        out_shape=[
            jax.ShapeDtypeStruct((tokens, features), F32),
            jax.ShapeDtypeStruct((tokens, features + 4 * tokens), BF16),
        ],
        scratch_shapes=held
        + [
            pltpu.VMEM((latent // 128, reqs * rows, 128), F32),
            pltpu.SemaphoreType.DMA((2 * reqs + 7,)),
        ],
        cost_estimate=pl.CostEstimate(
            flops=flops, bytes_accessed=6 * MIB, transcendentals=reqs * rows * slots
        ),
        compiler_params=pltpu.CompilerParams(vmem_limit_bytes=56 * MIB),
    )(*operands)


def dispatch_kernel(top, mine, here, there, high, low, *refs):
    blocks, table = refs[:-1], refs[-1]
    tokens, packed_rows = here.shape[0], blocks[0].shape[0]
    features = 2 * blocks[0].shape[1]
    here_routes, here_shares = unpacked(here.at[:, features:], top, tokens)
    there_routes, there_shares = unpacked(there.at[:, features:], top, tokens)
    routes = jnp.concatenate([here_routes, there_routes], axis=1)
    shares = jnp.concatenate([here_shares, there_shares], axis=1)
    experts = mine[...]
    both = 2 * tokens
    count = experts.shape[0]
    named = jnp.zeros((count, both), F32)
    weight = jnp.zeros((count, both), F32)
    for k in range(top):
        hit = jnp.where(routes[k : k + 1, :] == experts, 1.0, 0.0)
        named = named + hit
        weight = weight + hit * shares[k : k + 1, :]
    earlier = lax.broadcasted_iota(jnp.int32, (both, both), 0)
    later = lax.broadcasted_iota(jnp.int32, (both, both), 1)
    rank = jnp.dot(
        named.astype(BF16),
        jnp.where(earlier < later, 1.0, 0.0).astype(BF16),
        preferred_element_type=F32,
    ).astype(jnp.int32)
    full, rest = whole_tiles(packed_rows)
    places = [
        jnp.where(rank < full, q * full + rank, 2 * full + q * rest + rank - full)
        for q in range(2)
    ]
    place = jnp.concatenate([jnp.where(named > 0.0, p, -1) for p in places], axis=1)
    weight = jnp.concatenate([weight, weight], axis=1)
    slots = lax.broadcasted_iota(jnp.int32, (packed_rows, 2 * both), 0)
    middle = features // 2
    rows = jnp.concatenate(
        [r[:, q * middle : (q + 1) * middle] for q in range(2) for r in (here, there)], axis=0
    )
    for m, block in enumerate(blocks):
        hit = jnp.where(slots == place[m : m + 1, :], 1.0, 0.0)
        table[packed_rows * m : packed_rows * (m + 1), :] = hit * weight[m : m + 1, :]
        block[...] = jnp.dot(hit.astype(BF16), rows, preferred_element_type=F32).astype(BF16)
    turned = table[...].T
    top_bits = turned.astype(BF16)
    high[...] = top_bits
    low[...] = (turned - top_bits.astype(F32)).astype(BF16)


def whole_tiles(packed_rows):
    full = packed_rows // 2 // 8 * 8
    return full, packed_rows // 2 - full


def dispatch(mine, here, there, top, capacity):
    count, both = mine.shape[0], 2 * here.shape[0]
    width = here.shape[1] - 2 * both
    size = 4 * capacity
    return pl.pallas_call(
        functools.partial(dispatch_kernel, top),
        in_specs=[whole()] * 3,
        out_specs=[whole()] * (2 + count),
        out_shape=[jax.ShapeDtypeStruct((2 * both, count * size), BF16)] * 2
        + [jax.ShapeDtypeStruct((size, width // 2), BF16)] * count,
        scratch_shapes=[pltpu.VMEM((count * size, 2 * both), F32)],
        cost_estimate=pl.CostEstimate(
            flops=2 * count * size * both * width, bytes_accessed=3 * MIB // 2, transcendentals=0
        ),
        compiler_params=pltpu.CompilerParams(vmem_limit_bytes=16 * MIB),
    )(mine, here, there)


def load_kernel(*refs):
    count = len(refs) // 2
    sems = refs[-1]
    copies = [
        pltpu.make_async_copy(refs[i], refs[count + i], sems.at[i]) for i in range(count)
    ]
    for copy in copies:
        copy.start()
    for copy in copies:
        copy.wait()


def load(weights, room):
    return pl.pallas_call(
        load_kernel,
        in_specs=[pl.BlockSpec(memory_space=pl.ANY)] * len(weights),
        out_specs=[whole()] * len(weights),
        out_shape=[jax.ShapeDtypeStruct(w.shape, w.dtype) for w in weights],
        scratch_shapes=[pltpu.SemaphoreType.DMA((len(weights),))],
        cost_estimate=pl.CostEstimate(
            flops=0, bytes_accessed=2 * sum(2 * w.size for w in weights), transcendentals=0
        ),
        compiler_params=pltpu.CompilerParams(vmem_limit_bytes=room * MIB),
    )(*weights)


def expert_kernel(count, *refs):
    blocks, weights = refs[:count], refs[count : count + 6]
    outs = refs[count + 6 : 2 * count + 6]
    rows, active = refs[2 * count + 6 :]
    size, middle = blocks[0].shape
    full, rest = whole_tiles(size)
    given = [block[...].astype(F32) for block in blocks]
    for q in range(2):
        parts = [g[q * full : (q + 1) * full] for g in given]
        if rest:
            parts += [
                joined(*[g[2 * full :] for g in given[m : m + 2]])[q] for m in range(0, count, 2)
            ]
        rows[:, q * middle : (q + 1) * middle] = jnp.concatenate(parts, axis=0).astype(BF16)
    for half in range(2):
        w_gate, w_up = weights[3 * half : 3 * half + 2]
        gate = lax.dot_general(rows[...], w_gate[...], NT, preferred_element_type=F32)
        upper = lax.dot_general(rows[...], w_up[...], NT, preferred_element_type=F32)
        active[half] = (gate * (1.0 / (1.0 + jnp.exp(-gate))) * upper).astype(BF16)
    step = 256
    for at in range(0, middle, step):
        made = []
        for q in range(2):
            columns = slice(q * middle + at, q * middle + at + step)
            result = jnp.dot(active[0], weights[2][:, columns], preferred_element_type=F32)
            made.append(
                result + jnp.dot(active[1], weights[5][:, columns], preferred_element_type=F32)
            )
        for m, out in enumerate(outs):
            parts = [r[m * full : (m + 1) * full] for r in made]
            if rest:
                first = count * full + m // 2 * 8
                parts.append(joined(*[r[first : first + 8] for r in made])[m % 2])
            out[:, at : at + step] = jnp.concatenate(parts, axis=0).astype(BF16)


def joined(one, two):
    upper = lax.broadcasted_iota(jnp.int32, one.shape, 0) < 4
    return (
        jnp.where(upper, one, pltpu.roll(two, 4, 0)),
        jnp.where(upper, pltpu.roll(one, 4, 0), two),
    )


def run_expert(blocks, weights):
    count = len(blocks)
    size, middle = blocks[0].shape
    units, width = weights[0].shape
    rows = count * size // 2
    return pl.pallas_call(
        functools.partial(expert_kernel, count),
        in_specs=[whole()] * (count + 6),
        out_specs=[whole()] * count,
        out_shape=[jax.ShapeDtypeStruct((size, middle), BF16)] * count,
        scratch_shapes=[
            pltpu.VMEM((rows, width), BF16),
            pltpu.VMEM((2, rows, units), BF16),
        ],
        cost_estimate=pl.CostEstimate(
            flops=12 * rows * width * units,
            bytes_accessed=12 * units * width,
            transcendentals=2 * rows * units,
        ),
        compiler_params=pltpu.CompilerParams(vmem_limit_bytes=20 * MIB),
    )(*blocks, *weights)


def combine_kernel(high, low, *refs):
    blocks, (here, there) = refs[:-2], refs[-2:]
    rows = jnp.concatenate([block[...] for block in blocks], axis=0)
    total = jnp.dot(high[...], rows, preferred_element_type=F32)
    total = total + jnp.dot(low[...], rows, preferred_element_type=F32)
    tokens, middle = here.shape[0], rows.shape[1]
    for q in range(2):
        columns = slice(q * middle, (q + 1) * middle)
        here[:, columns] = total[2 * q * tokens : (2 * q + 1) * tokens]
        there[:, columns] = total[(2 * q + 1) * tokens : 2 * (q + 1) * tokens].astype(BF16)


def combine(high, low, blocks):
    both, width = high.shape[0] // 2, 2 * blocks[0].shape[1]
    return pl.pallas_call(
        combine_kernel,
        in_specs=[whole()] * (2 + len(blocks)),
        out_specs=[whole()] * 2,
        out_shape=[
            jax.ShapeDtypeStruct((both // 2, width), F32),
            jax.ShapeDtypeStruct((both // 2, width), BF16),
        ],
        cost_estimate=pl.CostEstimate(
            flops=2 * high.size * width, bytes_accessed=3 * MIB // 2, transcendentals=0
        ),
        compiler_params=pltpu.CompilerParams(vmem_limit_bytes=16 * MIB),
    )(high, low, *blocks)


def local(
    queries,
    cache,
    drafts,
    lengths,
    value_up,
    residual,
    norm_gain,
    w_gate,
    w_up,
    w_down,
    routes,
    combine_weights,
):
    tokens, top = routes.shape
    devices = lax.axis_size("ep")
    experts = devices // 2
    near = experts // 2
    capacity = min(tokens, 2 * (((tokens * top + experts - 1) // experts + 3) // 2))

    own = [jnp.swapaxes(w_gate, 1, 2)[0], jnp.swapaxes(w_up, 1, 2)[0], w_down[0]]
    other = [swapped(w, 1) for w in own]
    chip, core = lax.axis_index("ep") // 2, lax.axis_index("ep") % 2
    masks = jnp.where(core == 0, *[jnp.array(order, jnp.int32) for order in orders(near)])
    mine = (chip ^ masks).astype(F32)[:, None]

    stream, normed = attend(
        queries, cache, drafts, lengths, value_up, residual, norm_gain, routes.T, combine_weights.T
    )
    normed, own = lax.optimization_barrier((normed, own))
    across = swapped(normed, devices // 2)
    own = load(own, 44)
    across, own, other = lax.optimization_barrier((across, own, other))
    high, low, *blocks = dispatch(mine, normed, across, top, capacity)
    blocks = exchanged(blocks)
    blocks[2], *late = lax.optimization_barrier((blocks[2], *other[1:]))
    blocks = exchanged(run_expert(blocks, [*own, other[0], *load(late, 38)]))
    here, there = combine(high, low, blocks)
    return (stream + (here + swapped(there, devices // 2).astype(F32))).astype(BF16)


def solution(mesh):
    placed = (
        P(("groups", "ep"), None, None, None),
        P(("groups", "ep"), None, None),
        P(("groups", "ep"), None, None),
        P(("groups", "ep")),
        P(),
        P(("groups", "ep"), None),
        P(),
        P("ep", None, None),
        P("ep", None, None),
        P("ep", None, None),
        P(("groups", "ep"), None),
        P(("groups", "ep"), None),
    )
    return jax.shard_map(
        local, mesh=mesh, in_specs=placed, out_specs=P(("groups", "ep"), None), check_vma=False
    )
```

```python
import functools

import jax
import jax.numpy as jnp
from jax import lax
from jax.experimental import pallas as pl
from jax.experimental.pallas import tpu as pltpu
from jax.sharding import PartitionSpec as P

F32 = jnp.float32
BF16 = jnp.bfloat16
NT = (((1,), (1,)), ((), ()))
MIB = 1 << 20


def swapped(value, mask):
    pairs = [(source, source ^ mask) for source in range(lax.axis_size("ep"))]
    return lax.ppermute(value, "ep", pairs)


def orders(near):
    last = near - 1
    first = list(range(last, 0, -1))
    for i in (0, near // 2 - 1):
        first[i], first[i + 1] = first[i + 1], first[i]
    second = [m if m == last else last ^ m for m in first]
    return [*first, 0], [*second, 0]


def exchanged(blocks):
    got = list(blocks)
    for i, masks in enumerate(zip(*orders(len(blocks)))):
        pairs = [(d, d ^ 2 * masks[d % 2]) for d in range(lax.axis_size("ep"))]
        if any(masks):
            got[i] = lax.ppermute(blocks[i], "ep", pairs)
    return got


def whole():
    return pl.BlockSpec(memory_space=pltpu.VMEM)


def attend_kernel(heads, *refs):
    given, (stream, normed), held = refs[:9], refs[9:11], refs[11:20]
    mixed, sems = refs[20:]
    lengths, drafts, queries, cache, up, residual, gain, routes, shares = held
    reqs, rows, width = queries.shape
    slots = given[3].shape[2]
    draft = drafts.shape[1]
    latent, vdim = up.shape[1:]
    lanes = mixed.shape[2]
    columns = cache.shape[2]
    copies = {}
    order = [(0, None), (1, None)] + [(i, r) for r in range(reqs) for i in (2, 3)]
    for n, (i, r) in enumerate(order + [(i, None) for i in range(4, 9)]):
        source, target = (given[i], held[i]) if r is None else (given[i].at[r], held[i].at[r])
        if i == 3:
            target = target.at[:, :slots]
        copies[i, r] = pltpu.make_async_copy(source, target, sems.at[n])
        copies[i, r].start()
    scale = (vdim + width - latent) ** (-0.5)
    place = lax.broadcasted_iota(jnp.int32, (rows, columns), 1)
    token = lax.broadcasted_iota(jnp.int32, (rows, columns), 0) // heads
    causal = (place >= slots) & (place - slots <= token)
    copies[0, None].wait()
    copies[1, None].wait()
    for r in range(reqs):
        d = jnp.concatenate(
            [drafts[r].astype(F32), jnp.zeros((columns - slots - draft, width), F32)], axis=0
        )
        cache[r, :, slots:] = d.T.astype(BF16)
    for start in range(0, reqs, 2):
        some = range(start, min(reqs, start + 2))
        scores, probs = {}, {}
        for r in some:
            copies[2, r].wait()
            copies[3, r].wait()
        for r in some:
            score = jnp.dot(queries[r], cache[r], preferred_element_type=F32) * scale
            scores[r] = jnp.where((place < lengths[r]) | causal, score, -1e30)
        for r in some:
            e = jnp.exp(scores[r] - jnp.max(scores[r], axis=-1, keepdims=True))
            probs[r] = (e * (1.0 / jnp.sum(e, axis=-1, keepdims=True))).astype(BF16)
        for r in some:
            out = lax.dot_general(
                probs[r], cache[r, :latent, :], NT, preferred_element_type=F32
            )
            for g in range(latent // lanes):
                mixed[g, r * rows : (r + 1) * rows, :] = out[:, g * lanes : (g + 1) * lanes]
    for i in range(4, 9):
        copies[i, None].wait()
    tokens, features = stream.shape
    square = jnp.zeros((tokens, vdim), F32)
    for head in range(heads):
        part = jnp.concatenate(
            [mixed[g, pl.ds(head, tokens, stride=heads), :] for g in range(latent // lanes)],
            axis=1,
        ).astype(BF16)
        at = slice(head * vdim, (head + 1) * vdim)
        value = residual[:, at].astype(F32) + jnp.dot(
            part, up[head], preferred_element_type=F32
        )
        stream[:, at] = value
        square = square + value * value
    mean = jnp.sum(square, axis=-1, keepdims=True) / features
    factor = lax.rsqrt(mean + 1e-06)
    normed[:, :features] = (stream[...] * factor * gain[...]).astype(BF16)
    normed[:, features:] = packed(routes[...], shares[...], tokens)


def packed(routes, shares, tokens):
    top = routes.shape[0]
    first = shares.astype(BF16).astype(F32)
    second = (shares - first).astype(BF16).astype(F32)
    third = shares - first - second
    rows = jnp.concatenate([routes.astype(F32), first, second, third], axis=1)
    rest = jnp.zeros((tokens - top, rows.shape[1]), F32)
    return jnp.concatenate([rows, rest], axis=0).astype(BF16)


def unpacked(block, top, tokens):
    rows = block[...].astype(F32)[:top]
    parts = [rows[:, i * tokens : (i + 1) * tokens] for i in range(4)]
    return parts[0], parts[1] + parts[2] + parts[3]


def attend(queries, cache, drafts, lengths, value_up, residual, norm_gain, routes, shares):
    reqs, draft, heads, width = queries.shape
    slots = cache.shape[1]
    latent, vdim = value_up.shape[1:]
    tokens, features = residual.shape
    rows = draft * heads
    flops = 2 * reqs * rows * slots * (width + latent) + 2 * tokens * heads * latent * vdim
    operands = (
        lengths,
        drafts,
        queries.reshape(reqs, rows, width),
        jnp.swapaxes(cache, 1, 2),
        value_up,
        residual,
        norm_gain.reshape(1, features),
        routes,
        shares,
    )
    held = [pltpu.VMEM(o.shape, o.dtype) for o in operands]
    held[0] = pltpu.SMEM(lengths.shape, jnp.int32)
    held[3] = pltpu.VMEM((reqs, width, (slots + draft + 127) // 128 * 128), BF16)
    return pl.pallas_call(
        functools.partial(attend_kernel, heads),
        in_specs=[pl.BlockSpec(memory_space=pltpu.HBM)] * 9,
        out_specs=[whole()] * 2,
        out_shape=[
            jax.ShapeDtypeStruct((tokens, features), F32),
            jax.ShapeDtypeStruct((tokens, features + 4 * tokens), BF16),
        ],
        scratch_shapes=held
        + [
            pltpu.VMEM((latent // 128, reqs * rows, 128), F32),
            pltpu.SemaphoreType.DMA((2 * reqs + 7,)),
        ],
        cost_estimate=pl.CostEstimate(
            flops=flops, bytes_accessed=6 * MIB, transcendentals=reqs * rows * slots
        ),
        compiler_params=pltpu.CompilerParams(vmem_limit_bytes=56 * MIB),
    )(*operands)


def dispatch_kernel(top, mine, here, there, high, low, *refs):
    blocks, table = refs[:-1], refs[-1]
    tokens, packed_rows = here.shape[0], blocks[0].shape[0]
    features = 2 * blocks[0].shape[1]
    here_routes, here_shares = unpacked(here.at[:, features:], top, tokens)
    there_routes, there_shares = unpacked(there.at[:, features:], top, tokens)
    routes = jnp.concatenate([here_routes, there_routes], axis=1)
    shares = jnp.concatenate([here_shares, there_shares], axis=1)
    experts = mine[...]
    both = 2 * tokens
    count = experts.shape[0]
    named = jnp.zeros((count, both), F32)
    weight = jnp.zeros((count, both), F32)
    for k in range(top):
        hit = jnp.where(routes[k : k + 1, :] == experts, 1.0, 0.0)
        named = named + hit
        weight = weight + hit * shares[k : k + 1, :]
    earlier = lax.broadcasted_iota(jnp.int32, (both, both), 0)
    later = lax.broadcasted_iota(jnp.int32, (both, both), 1)
    rank = jnp.dot(
        named.astype(BF16),
        jnp.where(earlier < later, 1.0, 0.0).astype(BF16),
        preferred_element_type=F32,
    ).astype(jnp.int32)
    full, rest = whole_tiles(packed_rows)
    places = [
        jnp.where(rank < full, q * full + rank, 2 * full + q * rest + rank - full)
        for q in range(2)
    ]
    place = jnp.concatenate([jnp.where(named > 0.0, p, -1) for p in places], axis=1)
    weight = jnp.concatenate([weight, weight], axis=1)
    slots = lax.broadcasted_iota(jnp.int32, (packed_rows, 2 * both), 0)
    middle = features // 2
    rows = jnp.concatenate(
        [r[:, q * middle : (q + 1) * middle] for q in range(2) for r in (here, there)], axis=0
    )
    for m, block in enumerate(blocks):
        hit = jnp.where(slots == place[m : m + 1, :], 1.0, 0.0)
        table[packed_rows * m : packed_rows * (m + 1), :] = hit * weight[m : m + 1, :]
        block[...] = jnp.dot(hit.astype(BF16), rows, preferred_element_type=F32).astype(BF16)
    turned = table[...].T
    top_bits = turned.astype(BF16)
    high[...] = top_bits
    low[...] = (turned - top_bits.astype(F32)).astype(BF16)


def whole_tiles(packed_rows):
    full = packed_rows // 2 // 8 * 8
    return full, packed_rows // 2 - full


def dispatch(mine, here, there, top, capacity):
    count, both = mine.shape[0], 2 * here.shape[0]
    width = here.shape[1] - 2 * both
    size = 4 * capacity
    return pl.pallas_call(
        functools.partial(dispatch_kernel, top),
        in_specs=[whole()] * 3,
        out_specs=[whole()] * (2 + count),
        out_shape=[jax.ShapeDtypeStruct((2 * both, count * size), BF16)] * 2
        + [jax.ShapeDtypeStruct((size, width // 2), BF16)] * count,
        scratch_shapes=[pltpu.VMEM((count * size, 2 * both), F32)],
        cost_estimate=pl.CostEstimate(
            flops=2 * count * size * both * width, bytes_accessed=3 * MIB // 2, transcendentals=0
        ),
        compiler_params=pltpu.CompilerParams(vmem_limit_bytes=16 * MIB),
    )(mine, here, there)


def load_kernel(*refs):
    count = len(refs) // 2
    sems = refs[-1]
    copies = [
        pltpu.make_async_copy(refs[i], refs[count + i], sems.at[i]) for i in range(count)
    ]
    for copy in copies:
        copy.start()
    for copy in copies:
        copy.wait()


def load(weights, room):
    return pl.pallas_call(
        load_kernel,
        in_specs=[pl.BlockSpec(memory_space=pl.ANY)] * len(weights),
        out_specs=[whole()] * len(weights),
        out_shape=[jax.ShapeDtypeStruct(w.shape, w.dtype) for w in weights],
        scratch_shapes=[pltpu.SemaphoreType.DMA((len(weights),))],
        cost_estimate=pl.CostEstimate(
            flops=0, bytes_accessed=2 * sum(2 * w.size for w in weights), transcendentals=0
        ),
        compiler_params=pltpu.CompilerParams(vmem_limit_bytes=room * MIB),
    )(*weights)


def expert_kernel(count, *refs):
    blocks, weights = refs[:count], refs[count : count + 6]
    outs = refs[count + 6 : 2 * count + 6]
    rows, active = refs[2 * count + 6 :]
    size, middle = blocks[0].shape
    full, rest = whole_tiles(size)
    given = [block[...].astype(F32) for block in blocks]
    for q in range(2):
        parts = [g[q * full : (q + 1) * full] for g in given]
        if rest:
            parts += [
                joined(*[g[2 * full :] for g in given[m : m + 2]])[q] for m in range(0, count, 2)
            ]
        rows[:, q * middle : (q + 1) * middle] = jnp.concatenate(parts, axis=0).astype(BF16)
    for half in range(2):
        w_gate, w_up = weights[3 * half : 3 * half + 2]
        gate = lax.dot_general(rows[...], w_gate[...], NT, preferred_element_type=F32)
        upper = lax.dot_general(rows[...], w_up[...], NT, preferred_element_type=F32)
        active[half] = (gate * (1.0 / (1.0 + jnp.exp(-gate))) * upper).astype(BF16)
    step = 256
    for at in range(0, middle, step):
        made = []
        for q in range(2):
            columns = slice(q * middle + at, q * middle + at + step)
            result = jnp.dot(active[0], weights[2][:, columns], preferred_element_type=F32)
            made.append(
                result + jnp.dot(active[1], weights[5][:, columns], preferred_element_type=F32)
            )
        for m, out in enumerate(outs):
            parts = [r[m * full : (m + 1) * full] for r in made]
            if rest:
                first = count * full + m // 2 * 8
                parts.append(joined(*[r[first : first + 8] for r in made])[m % 2])
            out[:, at : at + step] = jnp.concatenate(parts, axis=0).astype(BF16)


def joined(one, two):
    upper = lax.broadcasted_iota(jnp.int32, one.shape, 0) < 4
    return (
        jnp.where(upper, one, pltpu.roll(two, 4, 0)),
        jnp.where(upper, pltpu.roll(one, 4, 0), two),
    )


def run_expert(blocks, weights):
    count = len(blocks)
    size, middle = blocks[0].shape
    units, width = weights[0].shape
    rows = count * size // 2
    return pl.pallas_call(
        functools.partial(expert_kernel, count),
        in_specs=[whole()] * (count + 6),
        out_specs=[whole()] * count,
        out_shape=[jax.ShapeDtypeStruct((size, middle), BF16)] * count,
        scratch_shapes=[
            pltpu.VMEM((rows, width), BF16),
            pltpu.VMEM((2, rows, units), BF16),
        ],
        cost_estimate=pl.CostEstimate(
            flops=12 * rows * width * units,
            bytes_accessed=12 * units * width,
            transcendentals=2 * rows * units,
        ),
        compiler_params=pltpu.CompilerParams(vmem_limit_bytes=20 * MIB),
    )(*blocks, *weights)


def combine_kernel(high, low, stream, *refs):
    blocks, (here, there) = refs[:-2], refs[-2:]
    rows = jnp.concatenate([block[...] for block in blocks], axis=0)
    total = jnp.dot(high[...], rows, preferred_element_type=F32)
    total = total + jnp.dot(low[...], rows, preferred_element_type=F32)
    tokens, middle = here.shape[0], rows.shape[1]
    for q in range(2):
        columns = slice(q * middle, (q + 1) * middle)
        mine = total[2 * q * tokens : (2 * q + 1) * tokens]
        here[:, columns] = stream[:, columns] + mine
        there[:, columns] = total[(2 * q + 1) * tokens : 2 * (q + 1) * tokens].astype(BF16)


def combine(high, low, stream, blocks):
    both, width = high.shape[0] // 2, 2 * blocks[0].shape[1]
    return pl.pallas_call(
        combine_kernel,
        in_specs=[whole()] * (3 + len(blocks)),
        out_specs=[whole()] * 2,
        out_shape=[
            jax.ShapeDtypeStruct((both // 2, width), F32),
            jax.ShapeDtypeStruct((both // 2, width), BF16),
        ],
        cost_estimate=pl.CostEstimate(
            flops=2 * high.size * width, bytes_accessed=3 * MIB // 2, transcendentals=0
        ),
        compiler_params=pltpu.CompilerParams(vmem_limit_bytes=16 * MIB),
    )(high, low, stream, *blocks)


def local(
    queries,
    cache,
    drafts,
    lengths,
    value_up,
    residual,
    norm_gain,
    w_gate,
    w_up,
    w_down,
    routes,
    combine_weights,
):
    tokens, top = routes.shape
    devices = lax.axis_size("ep")
    experts = devices // 2
    near = experts // 2
    capacity = min(tokens, 2 * (((tokens * top + experts - 1) // experts + 3) // 2))

    own = [jnp.swapaxes(w_gate, 1, 2)[0], jnp.swapaxes(w_up, 1, 2)[0], w_down[0]]
    other = [swapped(w, 1) for w in own]
    chip, core = lax.axis_index("ep") // 2, lax.axis_index("ep") % 2
    masks = jnp.where(core == 0, *[jnp.array(order, jnp.int32) for order in orders(near)])
    mine = (chip ^ masks).astype(F32)[:, None]

    stream, normed = attend(
        queries, cache, drafts, lengths, value_up, residual, norm_gain, routes.T, combine_weights.T
    )
    normed, own = lax.optimization_barrier((normed, own))
    across = swapped(normed, devices // 2)
    own = load(own, 44)
    across, own, other = lax.optimization_barrier((across, own, other))
    high, low, *blocks = dispatch(mine, normed, across, top, capacity)
    blocks = exchanged(blocks)
    blocks[2], *late = lax.optimization_barrier((blocks[2], *other[1:]))
    blocks = exchanged(run_expert(blocks, [*own, other[0], *load(late, 38)]))
    here, there = combine(high, low, stream, blocks)
    return (here + swapped(there, devices // 2).astype(F32)).astype(BF16)


def solution(mesh):
    placed = (
        P(("groups", "ep"), None, None, None),
        P(("groups", "ep"), None, None),
        P(("groups", "ep"), None, None),
        P(("groups", "ep")),
        P(),
        P(("groups", "ep"), None),
        P(),
        P("ep", None, None),
        P("ep", None, None),
        P("ep", None, None),
        P(("groups", "ep"), None),
        P(("groups", "ep"), None),
    )
    return jax.shard_map(
        local, mesh=mesh, in_specs=placed, out_specs=P(("groups", "ep"), None), check_vma=False
    )
```

```python
import functools

import jax
import jax.numpy as jnp
from jax import lax
from jax.experimental import pallas as pl
from jax.experimental.pallas import tpu as pltpu
from jax.sharding import PartitionSpec as P

F32 = jnp.float32
BF16 = jnp.bfloat16
NT = (((1,), (1,)), ((), ()))
MIB = 1 << 20


def swapped(value, mask):
    pairs = [(source, source ^ mask) for source in range(lax.axis_size("ep"))]
    return lax.ppermute(value, "ep", pairs)


def orders(near):
    last = near - 1
    first = list(range(last, 0, -1))
    for i in (0, near // 2 - 1, near - 3):
        first[i], first[i + 1] = first[i + 1], first[i]
    second = [m if m == last else last ^ m for m in first]
    return [*first, 0], [*second, 0]


def exchanged(blocks):
    got = list(blocks)
    for i, masks in enumerate(zip(*orders(len(blocks)))):
        pairs = [(d, d ^ 2 * masks[d % 2]) for d in range(lax.axis_size("ep"))]
        if any(masks):
            got[i] = lax.ppermute(blocks[i], "ep", pairs)
    return got


def whole():
    return pl.BlockSpec(memory_space=pltpu.VMEM)


def attend_kernel(heads, *refs):
    given, (stream, normed), held = refs[:9], refs[9:11], refs[11:20]
    mixed, sems = refs[20:]
    lengths, drafts, queries, cache, up, residual, gain, routes, shares = held
    reqs, rows, width = queries.shape
    slots = given[3].shape[2]
    draft = drafts.shape[1]
    latent, vdim = up.shape[1:]
    lanes = mixed.shape[2]
    columns = cache.shape[2]
    copies = {}
    order = [(0, None), (1, None)] + [(i, r) for r in range(reqs) for i in (2, 3)]
    for n, (i, r) in enumerate(order + [(i, None) for i in range(4, 9)]):
        source, target = (given[i], held[i]) if r is None else (given[i].at[r], held[i].at[r])
        if i == 3:
            target = target.at[:, :slots]
        copies[i, r] = pltpu.make_async_copy(source, target, sems.at[n])
        copies[i, r].start()
    scale = (vdim + width - latent) ** (-0.5)
    place = lax.broadcasted_iota(jnp.int32, (rows, columns), 1)
    token = lax.broadcasted_iota(jnp.int32, (rows, columns), 0) // heads
    causal = (place >= slots) & (place - slots <= token)
    copies[0, None].wait()
    copies[1, None].wait()
    for r in range(reqs):
        d = jnp.concatenate(
            [drafts[r].astype(F32), jnp.zeros((columns - slots - draft, width), F32)], axis=0
        )
        cache[r, :, slots:] = d.T.astype(BF16)
    for start in range(0, reqs, 2):
        some = range(start, min(reqs, start + 2))
        scores, probs = {}, {}
        for r in some:
            copies[2, r].wait()
            copies[3, r].wait()
        for r in some:
            score = jnp.dot(queries[r], cache[r], preferred_element_type=F32) * scale
            scores[r] = jnp.where((place < lengths[r]) | causal, score, -1e30)
        for r in some:
            e = jnp.exp(scores[r] - jnp.max(scores[r], axis=-1, keepdims=True))
            probs[r] = (e * (1.0 / jnp.sum(e, axis=-1, keepdims=True))).astype(BF16)
        for r in some:
            out = lax.dot_general(
                probs[r], cache[r, :latent, :], NT, preferred_element_type=F32
            )
            for g in range(latent // lanes):
                mixed[g, r * rows : (r + 1) * rows, :] = out[:, g * lanes : (g + 1) * lanes]
    for i in range(4, 9):
        copies[i, None].wait()
    tokens, features = stream.shape
    square = jnp.zeros((tokens, vdim), F32)
    for head in range(heads):
        part = jnp.concatenate(
            [mixed[g, pl.ds(head, tokens, stride=heads), :] for g in range(latent // lanes)],
            axis=1,
        ).astype(BF16)
        at = slice(head * vdim, (head + 1) * vdim)
        value = residual[:, at].astype(F32) + jnp.dot(
            part, up[head], preferred_element_type=F32
        )
        stream[:, at] = value
        square = square + value * value
    mean = jnp.sum(square, axis=-1, keepdims=True) / features
    factor = lax.rsqrt(mean + 1e-06)
    normed[:, :features] = (stream[...] * factor * gain[...]).astype(BF16)
    normed[:, features:] = packed(routes[...], shares[...], tokens)


def packed(routes, shares, tokens):
    top = routes.shape[0]
    first = shares.astype(BF16).astype(F32)
    second = (shares - first).astype(BF16).astype(F32)
    third = shares - first - second
    rows = jnp.concatenate([routes.astype(F32), first, second, third], axis=1)
    rest = jnp.zeros((tokens - top, rows.shape[1]), F32)
    return jnp.concatenate([rows, rest], axis=0).astype(BF16)


def unpacked(block, top, tokens):
    rows = block[...].astype(F32)[:top]
    parts = [rows[:, i * tokens : (i + 1) * tokens] for i in range(4)]
    return parts[0], parts[1] + parts[2] + parts[3]


def attend(queries, cache, drafts, lengths, value_up, residual, norm_gain, routes, shares):
    reqs, draft, heads, width = queries.shape
    slots = cache.shape[1]
    latent, vdim = value_up.shape[1:]
    tokens, features = residual.shape
    rows = draft * heads
    flops = 2 * reqs * rows * slots * (width + latent) + 2 * tokens * heads * latent * vdim
    operands = (
        lengths,
        drafts,
        queries.reshape(reqs, rows, width),
        jnp.swapaxes(cache, 1, 2),
        value_up,
        residual,
        norm_gain.reshape(1, features),
        routes,
        shares,
    )
    held = [pltpu.VMEM(o.shape, o.dtype) for o in operands]
    held[0] = pltpu.SMEM(lengths.shape, jnp.int32)
    held[3] = pltpu.VMEM((reqs, width, (slots + draft + 127) // 128 * 128), BF16)
    return pl.pallas_call(
        functools.partial(attend_kernel, heads),
        in_specs=[pl.BlockSpec(memory_space=pltpu.HBM)] * 9,
        out_specs=[whole()] * 2,
        out_shape=[
            jax.ShapeDtypeStruct((tokens, features), F32),
            jax.ShapeDtypeStruct((tokens, features + 4 * tokens), BF16),
        ],
        scratch_shapes=held
        + [
            pltpu.VMEM((latent // 128, reqs * rows, 128), F32),
            pltpu.SemaphoreType.DMA((2 * reqs + 7,)),
        ],
        cost_estimate=pl.CostEstimate(
            flops=flops, bytes_accessed=6 * MIB, transcendentals=reqs * rows * slots
        ),
        compiler_params=pltpu.CompilerParams(vmem_limit_bytes=56 * MIB),
    )(*operands)


def dispatch_kernel(top, mine, here, there, high, low, *refs):
    blocks, table = refs[:-1], refs[-1]
    tokens, packed_rows = here.shape[0], blocks[0].shape[0]
    features = 2 * blocks[0].shape[1]
    here_routes, here_shares = unpacked(here.at[:, features:], top, tokens)
    there_routes, there_shares = unpacked(there.at[:, features:], top, tokens)
    routes = jnp.concatenate([here_routes, there_routes], axis=1)
    shares = jnp.concatenate([here_shares, there_shares], axis=1)
    experts = mine[...]
    both = 2 * tokens
    count = experts.shape[0]
    named = jnp.zeros((count, both), F32)
    weight = jnp.zeros((count, both), F32)
    for k in range(top):
        hit = jnp.where(routes[k : k + 1, :] == experts, 1.0, 0.0)
        named = named + hit
        weight = weight + hit * shares[k : k + 1, :]
    earlier = lax.broadcasted_iota(jnp.int32, (both, both), 0)
    later = lax.broadcasted_iota(jnp.int32, (both, both), 1)
    rank = jnp.dot(
        named.astype(BF16),
        jnp.where(earlier < later, 1.0, 0.0).astype(BF16),
        preferred_element_type=F32,
    ).astype(jnp.int32)
    full, rest = whole_tiles(packed_rows)
    places = [
        jnp.where(rank < full, q * full + rank, 2 * full + q * rest + rank - full)
        for q in range(2)
    ]
    place = jnp.concatenate([jnp.where(named > 0.0, p, -1) for p in places], axis=1)
    weight = jnp.concatenate([weight, weight], axis=1)
    slots = lax.broadcasted_iota(jnp.int32, (packed_rows, 2 * both), 0)
    middle = features // 2
    rows = jnp.concatenate(
        [r[:, q * middle : (q + 1) * middle] for q in range(2) for r in (here, there)], axis=0
    )
    for m, block in enumerate(blocks):
        hit = jnp.where(slots == place[m : m + 1, :], 1.0, 0.0)
        table[packed_rows * m : packed_rows * (m + 1), :] = hit * weight[m : m + 1, :]
        block[...] = jnp.dot(hit.astype(BF16), rows, preferred_element_type=F32).astype(BF16)
    turned = table[...].T
    top_bits = turned.astype(BF16)
    high[...] = top_bits
    low[...] = (turned - top_bits.astype(F32)).astype(BF16)


def whole_tiles(packed_rows):
    full = packed_rows // 2 // 8 * 8
    return full, packed_rows // 2 - full


def dispatch(mine, here, there, top, capacity):
    count, both = mine.shape[0], 2 * here.shape[0]
    width = here.shape[1] - 2 * both
    size = 4 * capacity
    return pl.pallas_call(
        functools.partial(dispatch_kernel, top),
        in_specs=[whole()] * 3,
        out_specs=[whole()] * (2 + count),
        out_shape=[jax.ShapeDtypeStruct((2 * both, count * size), BF16)] * 2
        + [jax.ShapeDtypeStruct((size, width // 2), BF16)] * count,
        scratch_shapes=[pltpu.VMEM((count * size, 2 * both), F32)],
        cost_estimate=pl.CostEstimate(
            flops=2 * count * size * both * width, bytes_accessed=3 * MIB // 2, transcendentals=0
        ),
        compiler_params=pltpu.CompilerParams(vmem_limit_bytes=16 * MIB),
    )(mine, here, there)


def load_kernel(*refs):
    count = len(refs) // 2
    sems = refs[-1]
    copies = [
        pltpu.make_async_copy(refs[i], refs[count + i], sems.at[i]) for i in range(count)
    ]
    for copy in copies:
        copy.start()
    for copy in copies:
        copy.wait()


def load(weights, room):
    return pl.pallas_call(
        load_kernel,
        in_specs=[pl.BlockSpec(memory_space=pl.ANY)] * len(weights),
        out_specs=[whole()] * len(weights),
        out_shape=[jax.ShapeDtypeStruct(w.shape, w.dtype) for w in weights],
        scratch_shapes=[pltpu.SemaphoreType.DMA((len(weights),))],
        cost_estimate=pl.CostEstimate(
            flops=0, bytes_accessed=2 * sum(2 * w.size for w in weights), transcendentals=0
        ),
        compiler_params=pltpu.CompilerParams(vmem_limit_bytes=room * MIB),
    )(*weights)


def expert_kernel(count, *refs):
    blocks, weights = refs[:count], refs[count : count + 6]
    outs = refs[count + 6 : 2 * count + 6]
    rows, active = refs[2 * count + 6 :]
    size, middle = blocks[0].shape
    full, rest = whole_tiles(size)
    given = [block[...].astype(F32) for block in blocks]
    for q in range(2):
        parts = [g[q * full : (q + 1) * full] for g in given]
        if rest:
            parts += [
                joined(*[g[2 * full :] for g in given[m : m + 2]])[q] for m in range(0, count, 2)
            ]
        rows[:, q * middle : (q + 1) * middle] = jnp.concatenate(parts, axis=0).astype(BF16)
    for half in range(2):
        w_gate, w_up = weights[3 * half : 3 * half + 2]
        gate = lax.dot_general(rows[...], w_gate[...], NT, preferred_element_type=F32)
        upper = lax.dot_general(rows[...], w_up[...], NT, preferred_element_type=F32)
        active[half] = (gate * (1.0 / (1.0 + jnp.exp(-gate))) * upper).astype(BF16)
    step = 256
    for at in range(0, middle, step):
        made = []
        for q in range(2):
            columns = slice(q * middle + at, q * middle + at + step)
            result = jnp.dot(active[0], weights[2][:, columns], preferred_element_type=F32)
            made.append(
                result + jnp.dot(active[1], weights[5][:, columns], preferred_element_type=F32)
            )
        for m, out in enumerate(outs):
            parts = [r[m * full : (m + 1) * full] for r in made]
            if rest:
                first = count * full + m // 2 * 8
                parts.append(joined(*[r[first : first + 8] for r in made])[m % 2])
            out[:, at : at + step] = jnp.concatenate(parts, axis=0).astype(BF16)


def joined(one, two):
    upper = lax.broadcasted_iota(jnp.int32, one.shape, 0) < 4
    return (
        jnp.where(upper, one, pltpu.roll(two, 4, 0)),
        jnp.where(upper, pltpu.roll(one, 4, 0), two),
    )


def run_expert(blocks, weights):
    count = len(blocks)
    size, middle = blocks[0].shape
    units, width = weights[0].shape
    rows = count * size // 2
    return pl.pallas_call(
        functools.partial(expert_kernel, count),
        in_specs=[whole()] * (count + 6),
        out_specs=[whole()] * count,
        out_shape=[jax.ShapeDtypeStruct((size, middle), BF16)] * count,
        scratch_shapes=[
            pltpu.VMEM((rows, width), BF16),
            pltpu.VMEM((2, rows, units), BF16),
        ],
        cost_estimate=pl.CostEstimate(
            flops=12 * rows * width * units,
            bytes_accessed=12 * units * width,
            transcendentals=2 * rows * units,
        ),
        compiler_params=pltpu.CompilerParams(vmem_limit_bytes=20 * MIB),
    )(*blocks, *weights)


def combine_kernel(high, low, stream, *refs):
    blocks, (here, there) = refs[:-2], refs[-2:]
    rows = jnp.concatenate([block[...] for block in blocks], axis=0)
    total = jnp.dot(high[...], rows, preferred_element_type=F32)
    total = total + jnp.dot(low[...], rows, preferred_element_type=F32)
    tokens, middle = here.shape[0], rows.shape[1]
    for q in range(2):
        columns = slice(q * middle, (q + 1) * middle)
        mine = total[2 * q * tokens : (2 * q + 1) * tokens]
        here[:, columns] = stream[:, columns] + mine
        there[:, columns] = total[(2 * q + 1) * tokens : 2 * (q + 1) * tokens].astype(BF16)


def combine(high, low, stream, blocks):
    both, width = high.shape[0] // 2, 2 * blocks[0].shape[1]
    return pl.pallas_call(
        combine_kernel,
        in_specs=[whole()] * (3 + len(blocks)),
        out_specs=[whole()] * 2,
        out_shape=[
            jax.ShapeDtypeStruct((both // 2, width), F32),
            jax.ShapeDtypeStruct((both // 2, width), BF16),
        ],
        cost_estimate=pl.CostEstimate(
            flops=2 * high.size * width, bytes_accessed=3 * MIB // 2, transcendentals=0
        ),
        compiler_params=pltpu.CompilerParams(vmem_limit_bytes=16 * MIB),
    )(high, low, stream, *blocks)


def local(
    queries,
    cache,
    drafts,
    lengths,
    value_up,
    residual,
    norm_gain,
    w_gate,
    w_up,
    w_down,
    routes,
    combine_weights,
):
    tokens, top = routes.shape
    devices = lax.axis_size("ep")
    experts = devices // 2
    near = experts // 2
    capacity = min(tokens, 2 * (((tokens * top + experts - 1) // experts + 3) // 2))

    own = [jnp.swapaxes(w_gate, 1, 2)[0], jnp.swapaxes(w_up, 1, 2)[0], w_down[0]]
    other = [swapped(w, 1) for w in own]
    chip, core = lax.axis_index("ep") // 2, lax.axis_index("ep") % 2
    masks = jnp.where(core == 0, *[jnp.array(order, jnp.int32) for order in orders(near)])
    mine = (chip ^ masks).astype(F32)[:, None]

    stream, normed = attend(
        queries, cache, drafts, lengths, value_up, residual, norm_gain, routes.T, combine_weights.T
    )
    normed, own = lax.optimization_barrier((normed, own))
    across = swapped(normed, devices // 2)
    own = load(own, 44)
    across, own, *other[:2] = lax.optimization_barrier((across, own, *other[:2]))
    high, low, *blocks = dispatch(mine, normed, across, top, capacity)
    blocks = exchanged(blocks)
    blocks[2], *late = lax.optimization_barrier((blocks[2], *other[1:]))
    blocks = exchanged(run_expert(blocks, [*own, other[0], *load(late, 38)]))
    here, there = combine(high, low, stream, blocks)
    return (here + swapped(there, devices // 2).astype(F32)).astype(BF16)


def solution(mesh):
    placed = (
        P(("groups", "ep"), None, None, None),
        P(("groups", "ep"), None, None),
        P(("groups", "ep"), None, None),
        P(("groups", "ep")),
        P(),
        P(("groups", "ep"), None),
        P(),
        P("ep", None, None),
        P("ep", None, None),
        P("ep", None, None),
        P(("groups", "ep"), None),
        P(("groups", "ep"), None),
    )
    return jax.shard_map(
        local, mesh=mesh, in_specs=placed, out_specs=P(("groups", "ep"), None), check_vma=False
    )
```

```python
import functools

import jax
import jax.numpy as jnp
from jax import lax
from jax.experimental import pallas as pl
from jax.experimental.pallas import tpu as pltpu
from jax.sharding import PartitionSpec as P

F32 = jnp.float32
BF16 = jnp.bfloat16
NT = (((1,), (1,)), ((), ()))
MIB = 1 << 20


def swapped(value, mask):
    pairs = [(source, source ^ mask) for source in range(lax.axis_size("ep"))]
    return lax.ppermute(value, "ep", pairs)


def orders(near):
    last = near - 1
    first = list(range(last, 0, -1))
    for i in (0, near // 2 - 1, near - 3):
        first[i], first[i + 1] = first[i + 1], first[i]
    second = [m if m == last else last ^ m for m in first]
    return [*first, 0], [*second, 0]


def exchanged(blocks):
    got = list(blocks)
    for i, masks in enumerate(zip(*orders(len(blocks)))):
        pairs = [(d, d ^ 2 * masks[d % 2]) for d in range(lax.axis_size("ep"))]
        if any(masks):
            got[i] = lax.ppermute(blocks[i], "ep", pairs)
    return got


def whole():
    return pl.BlockSpec(memory_space=pltpu.VMEM)


def attend_kernel(heads, *refs):
    given, (stream, normed), held = refs[:9], refs[9:11], refs[11:20]
    mixed, sems = refs[20:]
    lengths, drafts, queries, cache, up, residual, gain, routes, shares = held
    reqs, rows, width = queries.shape
    slots = given[3].shape[2]
    draft = drafts.shape[1]
    latent, vdim = up.shape[1:]
    lanes = mixed.shape[2]
    columns = cache.shape[2]
    copies = {}
    order = [(0, None), (1, None)] + [(i, r) for r in range(reqs) for i in (2, 3)]
    for n, (i, r) in enumerate(order + [(i, None) for i in range(4, 9)]):
        source, target = (given[i], held[i]) if r is None else (given[i].at[r], held[i].at[r])
        if i == 3:
            target = target.at[:, :slots]
        copies[i, r] = pltpu.make_async_copy(source, target, sems.at[n])
        copies[i, r].start()
    scale = (vdim + width - latent) ** (-0.5)
    place = lax.broadcasted_iota(jnp.int32, (rows, columns), 1)
    token = lax.broadcasted_iota(jnp.int32, (rows, columns), 0) // heads
    causal = (place >= slots) & (place - slots <= token)
    copies[0, None].wait()
    copies[1, None].wait()
    for r in range(reqs):
        d = jnp.concatenate(
            [drafts[r].astype(F32), jnp.zeros((columns - slots - draft, width), F32)], axis=0
        )
        cache[r, :, slots:] = d.T.astype(BF16)
    for start in range(0, reqs, 2):
        some = range(start, min(reqs, start + 2))
        scores, probs = {}, {}
        for r in some:
            copies[2, r].wait()
            copies[3, r].wait()
        for r in some:
            score = jnp.dot(queries[r], cache[r], preferred_element_type=F32) * scale
            scores[r] = jnp.where((place < lengths[r]) | causal, score, -1e30)
        for r in some:
            e = jnp.exp(scores[r] - jnp.max(scores[r], axis=-1, keepdims=True))
            probs[r] = (e * (1.0 / jnp.sum(e, axis=-1, keepdims=True))).astype(BF16)
        for r in some:
            out = lax.dot_general(
                probs[r], cache[r, :latent, :], NT, preferred_element_type=F32
            )
            for g in range(latent // lanes):
                mixed[g, r * rows : (r + 1) * rows, :] = out[:, g * lanes : (g + 1) * lanes]
    for i in range(4, 9):
        copies[i, None].wait()
    tokens, features = stream.shape
    square = jnp.zeros((tokens, vdim), F32)
    for head in range(heads):
        part = jnp.concatenate(
            [mixed[g, pl.ds(head, tokens, stride=heads), :] for g in range(latent // lanes)],
            axis=1,
        ).astype(BF16)
        at = slice(head * vdim, (head + 1) * vdim)
        value = residual[:, at].astype(F32) + jnp.dot(
            part, up[head], preferred_element_type=F32
        )
        stream[:, at] = value
        square = square + value * value
    mean = jnp.sum(square, axis=-1, keepdims=True) / features
    factor = lax.rsqrt(mean + 1e-06)
    normed[:, :features] = (stream[...] * factor * gain[...]).astype(BF16)
    normed[:, features:] = packed(routes[...], shares[...], tokens)


def packed(routes, shares, tokens):
    top = routes.shape[0]
    first = shares.astype(BF16).astype(F32)
    second = (shares - first).astype(BF16).astype(F32)
    third = shares - first - second
    rows = jnp.concatenate([routes.astype(F32), first, second, third], axis=1)
    rest = jnp.zeros((tokens - top, rows.shape[1]), F32)
    return jnp.concatenate([rows, rest], axis=0).astype(BF16)


def unpacked(block, top, tokens):
    rows = block[...].astype(F32)[:top]
    parts = [rows[:, i * tokens : (i + 1) * tokens] for i in range(4)]
    return parts[0], parts[1] + parts[2] + parts[3]


def attend(queries, cache, drafts, lengths, value_up, residual, norm_gain, routes, shares):
    reqs, draft, heads, width = queries.shape
    slots = cache.shape[1]
    latent, vdim = value_up.shape[1:]
    tokens, features = residual.shape
    rows = draft * heads
    flops = 2 * reqs * rows * slots * (width + latent) + 2 * tokens * heads * latent * vdim
    operands = (
        lengths,
        drafts,
        queries.reshape(reqs, rows, width),
        jnp.swapaxes(cache, 1, 2),
        value_up,
        residual,
        norm_gain.reshape(1, features),
        routes,
        shares,
    )
    held = [pltpu.VMEM(o.shape, o.dtype) for o in operands]
    held[0] = pltpu.SMEM(lengths.shape, jnp.int32)
    held[3] = pltpu.VMEM((reqs, width, (slots + draft + 127) // 128 * 128), BF16)
    return pl.pallas_call(
        functools.partial(attend_kernel, heads),
        in_specs=[pl.BlockSpec(memory_space=pltpu.HBM)] * 9,
        out_specs=[whole()] * 2,
        out_shape=[
            jax.ShapeDtypeStruct((tokens, features), F32),
            jax.ShapeDtypeStruct((tokens, features + 4 * tokens), BF16),
        ],
        scratch_shapes=held
        + [
            pltpu.VMEM((latent // 128, reqs * rows, 128), F32),
            pltpu.SemaphoreType.DMA((2 * reqs + 7,)),
        ],
        cost_estimate=pl.CostEstimate(
            flops=flops, bytes_accessed=6 * MIB, transcendentals=reqs * rows * slots
        ),
        compiler_params=pltpu.CompilerParams(vmem_limit_bytes=56 * MIB),
    )(*operands)


def dispatch_kernel(top, mine, here, there, high, low, *refs):
    blocks, table = refs[:-1], refs[-1]
    tokens, packed_rows = here.shape[0], blocks[0].shape[0]
    features = 2 * blocks[0].shape[1]
    here_routes, here_shares = unpacked(here.at[:, features:], top, tokens)
    there_routes, there_shares = unpacked(there.at[:, features:], top, tokens)
    routes = jnp.concatenate([here_routes, there_routes], axis=1)
    shares = jnp.concatenate([here_shares, there_shares], axis=1)
    experts = mine[...]
    both = 2 * tokens
    count = experts.shape[0]
    named = jnp.zeros((count, both), F32)
    weight = jnp.zeros((count, both), F32)
    for k in range(top):
        hit = jnp.where(routes[k : k + 1, :] == experts, 1.0, 0.0)
        named = named + hit
        weight = weight + hit * shares[k : k + 1, :]
    earlier = lax.broadcasted_iota(jnp.int32, (both, both), 0)
    later = lax.broadcasted_iota(jnp.int32, (both, both), 1)
    rank = jnp.dot(
        named.astype(BF16),
        jnp.where(earlier < later, 1.0, 0.0).astype(BF16),
        preferred_element_type=F32,
    ).astype(jnp.int32)
    full, rest = whole_tiles(packed_rows)
    places = [
        jnp.where(rank < full, q * full + rank, 2 * full + q * rest + rank - full)
        for q in range(2)
    ]
    place = jnp.concatenate([jnp.where(named > 0.0, p, -1) for p in places], axis=1)
    weight = jnp.concatenate([weight, weight], axis=1)
    slots = lax.broadcasted_iota(jnp.int32, (packed_rows, 2 * both), 0)
    middle = features // 2
    rows = jnp.concatenate(
        [r[:, q * middle : (q + 1) * middle] for q in range(2) for r in (here, there)], axis=0
    )
    for m, block in enumerate(blocks):
        hit = jnp.where(slots == place[m : m + 1, :], 1.0, 0.0)
        table[packed_rows * m : packed_rows * (m + 1), :] = hit * weight[m : m + 1, :]
        block[...] = jnp.dot(hit.astype(BF16), rows, preferred_element_type=F32).astype(BF16)
    turned = table[...].T
    top_bits = turned.astype(BF16)
    high[...] = top_bits
    low[...] = (turned - top_bits.astype(F32)).astype(BF16)


def whole_tiles(packed_rows):
    full = packed_rows // 2 // 8 * 8
    return full, packed_rows // 2 - full


def dispatch(mine, here, there, top, capacity):
    count, both = mine.shape[0], 2 * here.shape[0]
    width = here.shape[1] - 2 * both
    size = 4 * capacity
    return pl.pallas_call(
        functools.partial(dispatch_kernel, top),
        in_specs=[whole()] * 3,
        out_specs=[whole()] * (2 + count),
        out_shape=[jax.ShapeDtypeStruct((2 * both, count * size), BF16)] * 2
        + [jax.ShapeDtypeStruct((size, width // 2), BF16)] * count,
        scratch_shapes=[pltpu.VMEM((count * size, 2 * both), F32)],
        cost_estimate=pl.CostEstimate(
            flops=2 * count * size * both * width, bytes_accessed=3 * MIB // 2, transcendentals=0
        ),
        compiler_params=pltpu.CompilerParams(vmem_limit_bytes=16 * MIB),
    )(mine, here, there)


def load_kernel(*refs):
    count = len(refs) // 2
    sems = refs[-1]
    copies = [
        pltpu.make_async_copy(refs[i], refs[count + i], sems.at[i]) for i in range(count)
    ]
    for copy in copies:
        copy.start()
    for copy in copies:
        copy.wait()


def load(weights, room):
    return pl.pallas_call(
        load_kernel,
        in_specs=[pl.BlockSpec(memory_space=pl.ANY)] * len(weights),
        out_specs=[whole()] * len(weights),
        out_shape=[jax.ShapeDtypeStruct(w.shape, w.dtype) for w in weights],
        scratch_shapes=[pltpu.SemaphoreType.DMA((len(weights),))],
        cost_estimate=pl.CostEstimate(
            flops=0, bytes_accessed=2 * sum(2 * w.size for w in weights), transcendentals=0
        ),
        compiler_params=pltpu.CompilerParams(vmem_limit_bytes=room * MIB),
    )(*weights)


def expert_kernel(count, *refs):
    blocks, weights = refs[:count], refs[count : count + 6]
    outs = refs[count + 6 : 2 * count + 6]
    rows, active = refs[2 * count + 6 :]
    size, middle = blocks[0].shape
    full, rest = whole_tiles(size)
    given = [block[...] for block in blocks]
    ends = [g[2 * full :].astype(F32) for g in given]
    for q in range(2):
        parts = [g[q * full : (q + 1) * full] for g in given]
        if rest:
            pairs = [joined(*ends[m : m + 2])[q] for m in range(0, count, 2)]
            parts.append(jnp.concatenate(pairs, axis=0).astype(BF16))
        rows[:, q * middle : (q + 1) * middle] = jnp.concatenate(parts, axis=0)
    for half in range(2):
        w_gate, w_up = weights[3 * half : 3 * half + 2]
        gate = lax.dot_general(rows[...], w_gate[...], NT, preferred_element_type=F32)
        upper = lax.dot_general(rows[...], w_up[...], NT, preferred_element_type=F32)
        active[half] = (gate * (1.0 / (1.0 + jnp.exp(-gate))) * upper).astype(BF16)
    step = 256
    for at in range(0, middle, step):
        made = []
        for q in range(2):
            columns = slice(q * middle + at, q * middle + at + step)
            result = jnp.dot(active[0], weights[2][:, columns], preferred_element_type=F32)
            made.append(
                result + jnp.dot(active[1], weights[5][:, columns], preferred_element_type=F32)
            )
        for m, out in enumerate(outs):
            parts = [r[m * full : (m + 1) * full] for r in made]
            if rest:
                first = count * full + m // 2 * 8
                parts.append(joined(*[r[first : first + 8] for r in made])[m % 2])
            out[:, at : at + step] = jnp.concatenate(parts, axis=0).astype(BF16)


def joined(one, two):
    upper = lax.broadcasted_iota(jnp.int32, one.shape, 0) < 4
    return (
        jnp.where(upper, one, pltpu.roll(two, 4, 0)),
        jnp.where(upper, pltpu.roll(one, 4, 0), two),
    )


def run_expert(blocks, weights):
    count = len(blocks)
    size, middle = blocks[0].shape
    units, width = weights[0].shape
    rows = count * size // 2
    return pl.pallas_call(
        functools.partial(expert_kernel, count),
        in_specs=[whole()] * (count + 6),
        out_specs=[whole()] * count,
        out_shape=[jax.ShapeDtypeStruct((size, middle), BF16)] * count,
        scratch_shapes=[
            pltpu.VMEM((rows, width), BF16),
            pltpu.VMEM((2, rows, units), BF16),
        ],
        cost_estimate=pl.CostEstimate(
            flops=12 * rows * width * units,
            bytes_accessed=12 * units * width,
            transcendentals=2 * rows * units,
        ),
        compiler_params=pltpu.CompilerParams(vmem_limit_bytes=20 * MIB),
    )(*blocks, *weights)


def combine_kernel(high, low, stream, *refs):
    blocks, (here, there) = refs[:-2], refs[-2:]
    rows = jnp.concatenate([block[...] for block in blocks], axis=0)
    both = high.shape[0]
    weights = jnp.concatenate([high[...], low[...]], axis=0)
    total = jnp.dot(weights, rows, preferred_element_type=F32)
    total = total[:both] + total[both:]
    tokens, middle = here.shape[0], rows.shape[1]
    for q in range(2):
        columns = slice(q * middle, (q + 1) * middle)
        mine = total[2 * q * tokens : (2 * q + 1) * tokens]
        here[:, columns] = stream[:, columns] + mine
        there[:, columns] = total[(2 * q + 1) * tokens : 2 * (q + 1) * tokens].astype(BF16)


def combine(high, low, stream, blocks):
    both, width = high.shape[0] // 2, 2 * blocks[0].shape[1]
    return pl.pallas_call(
        combine_kernel,
        in_specs=[whole()] * (3 + len(blocks)),
        out_specs=[whole()] * 2,
        out_shape=[
            jax.ShapeDtypeStruct((both // 2, width), F32),
            jax.ShapeDtypeStruct((both // 2, width), BF16),
        ],
        cost_estimate=pl.CostEstimate(
            flops=2 * high.size * width, bytes_accessed=3 * MIB // 2, transcendentals=0
        ),
        compiler_params=pltpu.CompilerParams(vmem_limit_bytes=16 * MIB),
    )(high, low, stream, *blocks)


def local(
    queries,
    cache,
    drafts,
    lengths,
    value_up,
    residual,
    norm_gain,
    w_gate,
    w_up,
    w_down,
    routes,
    combine_weights,
):
    tokens, top = routes.shape
    devices = lax.axis_size("ep")
    experts = devices // 2
    near = experts // 2
    capacity = min(tokens, 2 * (((tokens * top + experts - 1) // experts + 3) // 2))

    own = [jnp.swapaxes(w_gate, 1, 2)[0], jnp.swapaxes(w_up, 1, 2)[0], w_down[0]]
    other = [swapped(w, 1) for w in own]
    chip, core = lax.axis_index("ep") // 2, lax.axis_index("ep") % 2
    masks = jnp.where(core == 0, *[jnp.array(order, jnp.int32) for order in orders(near)])
    mine = (chip ^ masks).astype(F32)[:, None]

    stream, normed = attend(
        queries, cache, drafts, lengths, value_up, residual, norm_gain, routes.T, combine_weights.T
    )
    normed, own = lax.optimization_barrier((normed, own))
    across = swapped(normed, devices // 2)
    own = load(own, 44)
    across, own, *other[:2] = lax.optimization_barrier((across, own, *other[:2]))
    high, low, *blocks = dispatch(mine, normed, across, top, capacity)
    blocks = exchanged(blocks)
    blocks[2], *late = lax.optimization_barrier((blocks[2], *other[1:]))
    blocks = exchanged(run_expert(blocks, [*own, other[0], *load(late, 38)]))
    here, there = combine(high, low, stream, blocks)
    return (here + swapped(there, devices // 2).astype(F32)).astype(BF16)


def solution(mesh):
    placed = (
        P(("groups", "ep"), None, None, None),
        P(("groups", "ep"), None, None),
        P(("groups", "ep"), None, None),
        P(("groups", "ep")),
        P(),
        P(("groups", "ep"), None),
        P(),
        P("ep", None, None),
        P("ep", None, None),
        P("ep", None, None),
        P(("groups", "ep"), None),
        P(("groups", "ep"), None),
    )
    return jax.shard_map(
        local, mesh=mesh, in_specs=placed, out_specs=P(("groups", "ep"), None), check_vma=False
    )
```

```python
import functools

import jax
import jax.numpy as jnp
from jax import lax
from jax.experimental import pallas as pl
from jax.experimental.pallas import tpu as pltpu
from jax.sharding import PartitionSpec as P

F32 = jnp.float32
BF16 = jnp.bfloat16
NT = (((1,), (1,)), ((), ()))
MIB = 1 << 20


def swapped(value, mask):
    pairs = [(source, source ^ mask) for source in range(lax.axis_size("ep"))]
    return lax.ppermute(value, "ep", pairs)


def orders(near):
    last = near - 1
    first = list(range(last, 0, -1))
    for i in (0, near // 2 - 1, near - 3):
        first[i], first[i + 1] = first[i + 1], first[i]
    second = [m if m == last else last ^ m for m in first]
    return [*first, 0], [*second, 0]


def exchanged(blocks):
    got = list(blocks)
    for i, masks in enumerate(zip(*orders(len(blocks)))):
        pairs = [(d, d ^ 2 * masks[d % 2]) for d in range(lax.axis_size("ep"))]
        if any(masks):
            got[i] = lax.ppermute(blocks[i], "ep", pairs)
    return got


def whole():
    return pl.BlockSpec(memory_space=pltpu.VMEM)


def attend_kernel(heads, *refs):
    given, (stream, normed), held = refs[:9], refs[9:11], refs[11:20]
    mixed, sems = refs[20:]
    lengths, drafts, queries, cache, up, residual, gain, routes, shares = held
    reqs, rows, width = queries.shape
    slots = given[3].shape[2]
    draft = drafts.shape[1]
    latent, vdim = up.shape[1:]
    lanes = mixed.shape[2]
    columns = cache.shape[2]
    copies = {}
    order = [(0, None), (1, None)] + [(i, r) for r in range(reqs) for i in (2, 3)]
    for n, (i, r) in enumerate(order + [(i, None) for i in range(4, 9)]):
        source, target = (given[i], held[i]) if r is None else (given[i].at[r], held[i].at[r])
        if i == 3:
            target = target.at[:, :slots]
        copies[i, r] = pltpu.make_async_copy(source, target, sems.at[n])
        copies[i, r].start()
    scale = (vdim + width - latent) ** (-0.5)
    place = lax.broadcasted_iota(jnp.int32, (rows, columns), 1)
    token = lax.broadcasted_iota(jnp.int32, (rows, columns), 0) // heads
    causal = (place >= slots) & (place - slots <= token)
    copies[0, None].wait()
    copies[1, None].wait()
    for r in range(reqs):
        d = jnp.concatenate(
            [drafts[r].astype(F32), jnp.zeros((columns - slots - draft, width), F32)], axis=0
        )
        cache[r, :, slots:] = d.T.astype(BF16)
    for start in range(0, reqs, 4):
        some = range(start, min(reqs, start + 4))
        scores, probs = {}, {}
        for r in some:
            copies[2, r].wait()
            copies[3, r].wait()
            score = jnp.dot(queries[r], cache[r], preferred_element_type=F32) * scale
            scores[r] = jnp.where((place < lengths[r]) | causal, score, -1e30)
        for r in some:
            e = jnp.exp(scores[r] - jnp.max(scores[r], axis=-1, keepdims=True))
            probs[r] = (e * (1.0 / jnp.sum(e, axis=-1, keepdims=True))).astype(BF16)
        for r in some:
            out = lax.dot_general(
                probs[r], cache[r, :latent, :], NT, preferred_element_type=F32
            )
            for g in range(latent // lanes):
                mixed[g, r * rows : (r + 1) * rows, :] = out[:, g * lanes : (g + 1) * lanes]
    for i in range(4, 9):
        copies[i, None].wait()
    tokens, features = stream.shape
    square = jnp.zeros((tokens, vdim), F32)
    for head in range(heads):
        part = jnp.concatenate(
            [mixed[g, pl.ds(head, tokens, stride=heads), :] for g in range(latent // lanes)],
            axis=1,
        ).astype(BF16)
        at = slice(head * vdim, (head + 1) * vdim)
        value = residual[:, at].astype(F32) + jnp.dot(
            part, up[head], preferred_element_type=F32
        )
        stream[:, at] = value
        square = square + value * value
    mean = jnp.sum(square, axis=-1, keepdims=True) / features
    factor = lax.rsqrt(mean + 1e-06)
    normed[:, :features] = (stream[...] * factor * gain[...]).astype(BF16)
    normed[:, features:] = packed(routes[...], shares[...], tokens)


def packed(routes, shares, tokens):
    top = routes.shape[0]
    first = shares.astype(BF16).astype(F32)
    second = (shares - first).astype(BF16).astype(F32)
    third = shares - first - second
    rows = jnp.concatenate([routes.astype(F32), first, second, third], axis=1)
    rest = jnp.zeros((tokens - top, rows.shape[1]), F32)
    return jnp.concatenate([rows, rest], axis=0).astype(BF16)


def unpacked(block, top, tokens):
    rows = block[...].astype(F32)[:top]
    parts = [rows[:, i * tokens : (i + 1) * tokens] for i in range(4)]
    return parts[0], parts[1] + parts[2] + parts[3]


def attend(queries, cache, drafts, lengths, value_up, residual, norm_gain, routes, shares):
    reqs, draft, heads, width = queries.shape
    slots = cache.shape[1]
    latent, vdim = value_up.shape[1:]
    tokens, features = residual.shape
    rows = draft * heads
    flops = 2 * reqs * rows * slots * (width + latent) + 2 * tokens * heads * latent * vdim
    operands = (
        lengths,
        drafts,
        queries.reshape(reqs, rows, width),
        jnp.swapaxes(cache, 1, 2),
        value_up,
        residual,
        norm_gain.reshape(1, features),
        routes,
        shares,
    )
    held = [pltpu.VMEM(o.shape, o.dtype) for o in operands]
    held[0] = pltpu.SMEM(lengths.shape, jnp.int32)
    held[3] = pltpu.VMEM((reqs, width, (slots + draft + 127) // 128 * 128), BF16)
    return pl.pallas_call(
        functools.partial(attend_kernel, heads),
        in_specs=[pl.BlockSpec(memory_space=pltpu.HBM)] * 9,
        out_specs=[whole()] * 2,
        out_shape=[
            jax.ShapeDtypeStruct((tokens, features), F32),
            jax.ShapeDtypeStruct((tokens, features + 4 * tokens), BF16),
        ],
        scratch_shapes=held
        + [
            pltpu.VMEM((latent // 128, reqs * rows, 128), F32),
            pltpu.SemaphoreType.DMA((2 * reqs + 7,)),
        ],
        cost_estimate=pl.CostEstimate(
            flops=flops, bytes_accessed=6 * MIB, transcendentals=reqs * rows * slots
        ),
        compiler_params=pltpu.CompilerParams(vmem_limit_bytes=56 * MIB),
    )(*operands)


def dispatch_kernel(top, mine, here, there, high, low, *refs):
    blocks, table = refs[:-1], refs[-1]
    tokens, packed_rows = here.shape[0], blocks[0].shape[0]
    features = 2 * blocks[0].shape[1]
    here_routes, here_shares = unpacked(here.at[:, features:], top, tokens)
    there_routes, there_shares = unpacked(there.at[:, features:], top, tokens)
    routes = jnp.concatenate([here_routes, there_routes], axis=1)
    shares = jnp.concatenate([here_shares, there_shares], axis=1)
    experts = mine[...]
    both = 2 * tokens
    count = experts.shape[0]
    named = jnp.zeros((count, both), F32)
    weight = jnp.zeros((count, both), F32)
    for k in range(top):
        hit = jnp.where(routes[k : k + 1, :] == experts, 1.0, 0.0)
        named = named + hit
        weight = weight + hit * shares[k : k + 1, :]
    earlier = lax.broadcasted_iota(jnp.int32, (both, both), 0)
    later = lax.broadcasted_iota(jnp.int32, (both, both), 1)
    rank = jnp.dot(
        named.astype(BF16),
        jnp.where(earlier < later, 1.0, 0.0).astype(BF16),
        preferred_element_type=F32,
    ).astype(jnp.int32)
    full, rest = whole_tiles(packed_rows)
    places = [
        jnp.where(rank < full, q * full + rank, 2 * full + q * rest + rank - full)
        for q in range(2)
    ]
    place = jnp.concatenate([jnp.where(named > 0.0, p, -1) for p in places], axis=1)
    weight = jnp.concatenate([weight, weight], axis=1)
    slots = lax.broadcasted_iota(jnp.int32, (packed_rows, 2 * both), 0)
    middle = features // 2
    rows = jnp.concatenate(
        [r[:, q * middle : (q + 1) * middle] for q in range(2) for r in (here, there)], axis=0
    )
    for m, block in enumerate(blocks):
        hit = jnp.where(slots == place[m : m + 1, :], 1.0, 0.0)
        table[packed_rows * m : packed_rows * (m + 1), :] = hit * weight[m : m + 1, :]
        block[...] = jnp.dot(hit.astype(BF16), rows, preferred_element_type=F32).astype(BF16)
    turned = table[...].T
    top_bits = turned.astype(BF16)
    high[...] = top_bits
    low[...] = (turned - top_bits.astype(F32)).astype(BF16)


def whole_tiles(packed_rows):
    full = packed_rows // 2 // 8 * 8
    return full, packed_rows // 2 - full


def dispatch(mine, here, there, top, capacity):
    count, both = mine.shape[0], 2 * here.shape[0]
    width = here.shape[1] - 2 * both
    size = 4 * capacity
    return pl.pallas_call(
        functools.partial(dispatch_kernel, top),
        in_specs=[whole()] * 3,
        out_specs=[whole()] * (2 + count),
        out_shape=[jax.ShapeDtypeStruct((2 * both, count * size), BF16)] * 2
        + [jax.ShapeDtypeStruct((size, width // 2), BF16)] * count,
        scratch_shapes=[pltpu.VMEM((count * size, 2 * both), F32)],
        cost_estimate=pl.CostEstimate(
            flops=2 * count * size * both * width, bytes_accessed=3 * MIB // 2, transcendentals=0
        ),
        compiler_params=pltpu.CompilerParams(vmem_limit_bytes=16 * MIB),
    )(mine, here, there)


def load_kernel(*refs):
    count = len(refs) // 2
    sems = refs[-1]
    copies = [
        pltpu.make_async_copy(refs[i], refs[count + i], sems.at[i]) for i in range(count)
    ]
    for copy in copies:
        copy.start()
    for copy in copies:
        copy.wait()


def load(weights, room):
    return pl.pallas_call(
        load_kernel,
        in_specs=[pl.BlockSpec(memory_space=pl.ANY)] * len(weights),
        out_specs=[whole()] * len(weights),
        out_shape=[jax.ShapeDtypeStruct(w.shape, w.dtype) for w in weights],
        scratch_shapes=[pltpu.SemaphoreType.DMA((len(weights),))],
        cost_estimate=pl.CostEstimate(
            flops=0, bytes_accessed=2 * sum(2 * w.size for w in weights), transcendentals=0
        ),
        compiler_params=pltpu.CompilerParams(vmem_limit_bytes=room * MIB),
    )(*weights)


def expert_kernel(count, *refs):
    blocks, weights = refs[:count], refs[count : count + 6]
    outs = refs[count + 6 : 2 * count + 6]
    rows, active = refs[2 * count + 6 :]
    size, middle = blocks[0].shape
    full, rest = whole_tiles(size)
    given = [block[...] for block in blocks]
    ends = [g[2 * full :].astype(F32) for g in given]
    for q in range(2):
        parts = [g[q * full : (q + 1) * full] for g in given]
        if rest:
            pairs = [joined(*ends[m : m + 2])[q] for m in range(0, count, 2)]
            parts.append(jnp.concatenate(pairs, axis=0).astype(BF16))
        rows[:, q * middle : (q + 1) * middle] = jnp.concatenate(parts, axis=0)
    for half in range(2):
        w_gate, w_up = weights[3 * half : 3 * half + 2]
        gate = lax.dot_general(rows[...], w_gate[...], NT, preferred_element_type=F32)
        upper = lax.dot_general(rows[...], w_up[...], NT, preferred_element_type=F32)
        active[half] = (gate * (1.0 / (1.0 + jnp.exp(-gate))) * upper).astype(BF16)
    step = 256
    for at in range(0, middle, step):
        made = []
        for q in range(2):
            columns = slice(q * middle + at, q * middle + at + step)
            result = jnp.dot(active[0], weights[2][:, columns], preferred_element_type=F32)
            made.append(
                result + jnp.dot(active[1], weights[5][:, columns], preferred_element_type=F32)
            )
        for m, out in enumerate(outs):
            parts = [r[m * full : (m + 1) * full] for r in made]
            if rest:
                first = count * full + m // 2 * 8
                parts.append(joined(*[r[first : first + 8] for r in made])[m % 2])
            out[:, at : at + step] = jnp.concatenate(parts, axis=0).astype(BF16)


def joined(one, two):
    upper = lax.broadcasted_iota(jnp.int32, one.shape, 0) < 4
    return (
        jnp.where(upper, one, pltpu.roll(two, 4, 0)),
        jnp.where(upper, pltpu.roll(one, 4, 0), two),
    )


def run_expert(blocks, weights):
    count = len(blocks)
    size, middle = blocks[0].shape
    units, width = weights[0].shape
    rows = count * size // 2
    return pl.pallas_call(
        functools.partial(expert_kernel, count),
        in_specs=[whole()] * (count + 6),
        out_specs=[whole()] * count,
        out_shape=[jax.ShapeDtypeStruct((size, middle), BF16)] * count,
        scratch_shapes=[
            pltpu.VMEM((rows, width), BF16),
            pltpu.VMEM((2, rows, units), BF16),
        ],
        cost_estimate=pl.CostEstimate(
            flops=12 * rows * width * units,
            bytes_accessed=12 * units * width,
            transcendentals=2 * rows * units,
        ),
        compiler_params=pltpu.CompilerParams(vmem_limit_bytes=20 * MIB),
    )(*blocks, *weights)


def combine_kernel(high, low, stream, *refs):
    blocks, (here, there) = refs[:-2], refs[-2:]
    rows = jnp.concatenate([block[...] for block in blocks], axis=0)
    both = high.shape[0]
    weights = jnp.concatenate([high[...], low[...]], axis=0)
    total = jnp.dot(weights, rows, preferred_element_type=F32)
    total = total[:both] + total[both:]
    tokens, middle = here.shape[0], rows.shape[1]
    for q in range(2):
        columns = slice(q * middle, (q + 1) * middle)
        mine = total[2 * q * tokens : (2 * q + 1) * tokens]
        here[:, columns] = stream[:, columns] + mine
        there[:, columns] = total[(2 * q + 1) * tokens : 2 * (q + 1) * tokens].astype(BF16)


def combine(high, low, stream, blocks):
    both, width = high.shape[0] // 2, 2 * blocks[0].shape[1]
    return pl.pallas_call(
        combine_kernel,
        in_specs=[whole()] * (3 + len(blocks)),
        out_specs=[whole()] * 2,
        out_shape=[
            jax.ShapeDtypeStruct((both // 2, width), F32),
            jax.ShapeDtypeStruct((both // 2, width), BF16),
        ],
        cost_estimate=pl.CostEstimate(
            flops=2 * high.size * width, bytes_accessed=3 * MIB // 2, transcendentals=0
        ),
        compiler_params=pltpu.CompilerParams(vmem_limit_bytes=16 * MIB),
    )(high, low, stream, *blocks)


def local(
    queries,
    cache,
    drafts,
    lengths,
    value_up,
    residual,
    norm_gain,
    w_gate,
    w_up,
    w_down,
    routes,
    combine_weights,
):
    tokens, top = routes.shape
    devices = lax.axis_size("ep")
    experts = devices // 2
    near = experts // 2
    capacity = min(tokens, 2 * (((tokens * top + experts - 1) // experts + 3) // 2))

    own = [jnp.swapaxes(w_gate, 1, 2)[0], jnp.swapaxes(w_up, 1, 2)[0], w_down[0]]
    other = [swapped(w, 1) for w in own]
    chip, core = lax.axis_index("ep") // 2, lax.axis_index("ep") % 2
    masks = jnp.where(core == 0, *[jnp.array(order, jnp.int32) for order in orders(near)])
    mine = (chip ^ masks).astype(F32)[:, None]

    stream, normed = attend(
        queries, cache, drafts, lengths, value_up, residual, norm_gain, routes.T, combine_weights.T
    )
    normed, own = lax.optimization_barrier((normed, own))
    across = swapped(normed, devices // 2)
    own = load(own, 44)
    across, own, *other[:2] = lax.optimization_barrier((across, own, *other[:2]))
    high, low, *blocks = dispatch(mine, normed, across, top, capacity)
    blocks = exchanged(blocks)
    blocks[2], *late = lax.optimization_barrier((blocks[2], *other[1:]))
    blocks = exchanged(run_expert(blocks, [*own, other[0], *load(late, 38)]))
    here, there = combine(high, low, stream, blocks)
    return (here + swapped(there, devices // 2).astype(F32)).astype(BF16)


def solution(mesh):
    placed = (
        P(("groups", "ep"), None, None, None),
        P(("groups", "ep"), None, None),
        P(("groups", "ep"), None, None),
        P(("groups", "ep")),
        P(),
        P(("groups", "ep"), None),
        P(),
        P("ep", None, None),
        P("ep", None, None),
        P("ep", None, None),
        P(("groups", "ep"), None),
        P(("groups", "ep"), None),
    )
    return jax.shard_map(
        local, mesh=mesh, in_specs=placed, out_specs=P(("groups", "ep"), None), check_vma=False
    )
```
